32 devices in a mesh: groups: 2 (over y), seq: 4 (over z), tensor: 2 (over x), ctx: 2 (over core).
Axes of the slice: x: 2, y: 2, z: 4, core: 2. Of those that a mesh axis runs over, the one named last changes fastest.
Arguments:
- query_in: bfloat16 [8192, 4096], P(('groups', 'seq', 'ctx'), 'tensor'), parts along dimension 0, may hold values from -6 to 6
- key_in: bfloat16 [8192, 4096], P(('groups', 'seq', 'ctx'), 'tensor'), parts along dimension 0, may hold values from -6 to 6
- value_in: bfloat16 [8192, 4096], P(('groups', 'seq', 'ctx'), 'tensor'), parts along dimension 0, may hold values from -6 to 6
- log_decay: float32 [32, 8192], P('tensor', ('groups', 'seq', 'ctx')), parts along dimension 1, may hold values from -2 to 0
- doc_start: int32 [8192], P(('groups', 'seq', 'ctx')), parts along dimension 0, may hold values 0 or 1
- out_grad: bfloat16 [8192, 4096], P(('groups', 'seq', 'ctx'), 'tensor'), parts along dimension 0, may hold values from -6 to 6
Outputs:
- normed: bfloat16 [8192, 4096], P(('groups', 'seq', 'ctx'), 'tensor'), parts along dimension 0
- query_gradient: bfloat16 [8192, 4096], P(('groups', 'seq', 'ctx'), 'tensor'), parts along dimension 0
- key_gradient: bfloat16 [8192, 4096], P(('groups', 'seq', 'ctx'), 'tensor'), parts along dimension 0
- value_gradient: bfloat16 [8192, 4096], P(('groups', 'seq', 'ctx'), 'tensor'), parts along dimension 0
The draws below stay inside these ranges and needn't reach their ends.
There are 2 independent parts, one for each index of `groups`. The reference program is written for one: setup_inputs(seed, part) draws one part's arguments, and reference() takes and returns one part's arrays. A program takes and returns all parts, laid end to end along the dimension named above; each array names one. Nothing has to cross between parts.
All inputs are finite; a program needn't handle non-finite values. No bound on the sum of `doc_start` on one device may be relied on, other than what follows from the above.
Results may differ from the reference program's by a relative error of at most 0.0071.
Values sent between devices are 32-bit elements; how exact they have to be, the bound alone decides.
No kernel may reach another device: no remote copies, remote signals or barrier semaphores. Data moves between devices by JAX's collectives and lax.ppermute only.
A program may use at most 128 MiB of HBM per device.

```python
import math
import jax
import jax.numpy as jnp
from jax import lax

HEAD_TOTAL = 32
DH = 128
BLOCK = 512
T_DEV = 512
PACKED_TOKENS = 4096


def run_levels(key):
    level_key = jax.random.fold_in(key, 41)
    pick_key, quiet_key, loud_key = jax.random.split(level_key, 3)
    runs = PACKED_TOKENS // T_DEV
    quiet = jax.random.uniform(pick_key, (runs, HEAD_TOTAL)) < 0.4
    small = jnp.exp(jax.random.uniform(quiet_key, (runs, HEAD_TOTAL), minval=math.log(0.06), maxval=math.log(0.12)))
    large = jnp.exp(jax.random.uniform(loud_key, (runs, HEAD_TOTAL), minval=math.log(0.7), maxval=math.log(1.4)))
    return jnp.where(quiet, small, large)


def leveled_rows(levels, key, spread_low, spread_high):
    runs = PACKED_TOKENS // T_DEV
    shape = (runs, T_DEV, HEAD_TOTAL, DH)
    noise = jnp.clip(jax.random.normal(key, shape), -6.0, 6.0)
    scaled = jnp.clip(noise * levels[:, None, :, None], spread_low, spread_high)
    return scaled.reshape(PACKED_TOKENS, HEAD_TOTAL * DH).astype(jnp.bfloat16)


def draw_key_in(key, part):
    levels = run_levels(key)
    key = jax.random.fold_in(key, 11)
    return leveled_rows(levels, key, -6.0, 6.0)


def draw_value_in(key, part):
    levels = run_levels(key)
    key = jax.random.fold_in(key, 13)
    return leveled_rows(levels, key, -6.0, 6.0)


def draw_log_decay(key, part):
    key = jax.random.fold_in(key, 7)
    sequence_lanes = jax.random.split(key, 8)
    fast_share = 0.3
    middle_share = 0.35
    random_noise = jnp.exp(jax.random.uniform(sequence_lanes[3], (HEAD_TOTAL, PACKED_TOKENS), minval=-0.7, maxval=0.7))
    head_pick = jax.random.uniform(sequence_lanes[0], (HEAD_TOTAL,))
    fast_rate = jnp.exp(jax.random.uniform(sequence_lanes[1], (HEAD_TOTAL,), minval=math.log(1.0 / 50.0), maxval=math.log(1.0 / 30.0)))
    middle_rate = jax.random.uniform(sequence_lanes[7], (HEAD_TOTAL,), minval=3.0, maxval=5.5) / T_DEV
    slow_rate = jnp.exp(jax.random.uniform(sequence_lanes[2], (HEAD_TOTAL,), minval=math.log(0.05), maxval=math.log(0.5))) / PACKED_TOKENS
    head_decay_rates = jnp.where(head_pick < fast_share, fast_rate, jnp.where(head_pick < fast_share + middle_share, middle_rate, slow_rate))
    segment_index = jnp.repeat(jnp.exp(jax.random.uniform(sequence_lanes[4], (HEAD_TOTAL, PACKED_TOKENS // BLOCK), minval=-0.5, maxval=0.5)), BLOCK, axis=1)
    break_positions = jax.random.randint(sequence_lanes[5], (HEAD_TOTAL, 2), 0, PACKED_TOKENS)
    loss_values = jax.random.uniform(sequence_lanes[6], (HEAD_TOTAL, 2), minval=0.2, maxval=0.5)
    document_breaks = break_positions[:, :, None] == jnp.arange(PACKED_TOKENS)[None, None, :]
    document_spans = jnp.sum(jnp.where(document_breaks, jnp.log1p(-loss_values)[:, :, None], 0.0), axis=1)
    combined = -head_decay_rates[:, None] * random_noise * segment_index + document_spans
    return jnp.clip(combined, -2.0, 0.0).astype(jnp.float32)


def place_ends(drawn, rng, least, largest):
    extent = drawn.shape
    index_at = [jax.random.randint(jax.random.fold_in(rng, axis), (), 0, extent[axis]) for axis in range(len(extent))]
    drawn = drawn.at[tuple(index_at)].set(least)
    longest = extent.index(max(extent))
    index_at[longest] = (index_at[longest] + 1) % extent[longest]
    return drawn.at[tuple(index_at)].set(largest)


def shard_levels(key, dims, pieces, least, high):
    factor_of, own = 1.0, jax.random.fold_in(key, 6)
    for dim, shards_of in pieces:
        heights = jnp.exp(jax.random.uniform(jax.random.fold_in(own, dim), (shards_of,), jnp.float32, least / len(pieces), high / len(pieces)))
        factor_of = factor_of * jnp.repeat(heights, dims[dim] // shards_of).reshape([-1 if axis == dim else 1 for axis in range(len(dims))])
    return factor_of


def normal_values(stream_key, extent, width, limit, pieces=(), dtype=jnp.bfloat16):
    values = jax.random.normal(stream_key, extent, jnp.float32) * width
    if len(pieces) > 0:
        values = shard_levels(stream_key, extent, pieces, -0.22, 0.18) * values
    return jnp.clip(values, min=-limit, max=limit).astype(dtype)


def setup_inputs(seed: int = 0, part: int = 0) -> dict:
    arg_keys = jax.random.split(jax.random.key(seed), 7)
    part_keys = jax.random.split(jax.random.fold_in(arg_keys[6], part), 7)
    return {
        "query_in": normal_values(part_keys[0], (PACKED_TOKENS, HEAD_TOTAL * DH), 1.0, 6.0, ((0, 8), (1, 2))),
        "key_in": draw_key_in(jax.random.fold_in(jax.random.fold_in(arg_keys[6], part), 71), part),
        "value_in": draw_value_in(jax.random.fold_in(jax.random.fold_in(arg_keys[6], part), 71), part),
        "log_decay": draw_log_decay(jax.random.fold_in(jax.random.fold_in(arg_keys[6], part), 71), part),
        "doc_start": place_ends((jax.random.randint(part_keys[4], (PACKED_TOKENS,), 0, 2 * T_DEV) < 1).astype(jnp.int32), jax.random.fold_in(part_keys[4], 1), 0, 1),
        "out_grad": normal_values(part_keys[5], (PACKED_TOKENS, HEAD_TOTAL * DH), 1.0, 6.0, ((0, 8), (1, 2))),
    }


EPS = 1e-06

def rounded_output(values_f32):
    return lax.optimization_barrier(values_f32.astype(jnp.bfloat16)).astype(jnp.float32)

def block_parts(log_rates, starts):
    cumulative = jnp.cumsum(log_rates, axis=1)
    documents = jnp.cumsum(starts)
    places = jnp.arange(BLOCK)
    causal = (documents[:, None] == documents[None, :]) & (places[:, None] >= places[None, :])
    spread = jnp.where(causal[None], cumulative[:, :, None] - cumulative[:, None, :], -1e+30)
    weights = jnp.exp(spread)
    entering_state = jnp.where(documents[None, :] == 0, jnp.exp(cumulative), 0.0)
    leaving_state = jnp.where(documents[None, :] == documents[-1], jnp.exp(cumulative[:, -1:] - cumulative), 0.0)
    passing = jnp.where(documents[-1] == 0, jnp.exp(cumulative[:, -1]), 0.0)
    return (weights, entering_state.T[:, :, None], leaving_state.T[:, :, None], passing)

def forward_block(carried_state, inputs):
    query_block, key_block, value_block, log_rates, starts = inputs
    weights, entering_state, leaving_state, passing = block_parts(log_rates, starts)
    query_single_float = query_block.astype(jnp.float32)
    key_single_float = key_block.astype(jnp.float32)
    value_single_float = value_block.astype(jnp.float32)
    attend_weights = rounded_output(jnp.einsum('thd,shd->hts', query_single_float, key_single_float) * weights)
    inside = jnp.einsum('cnr,rco->nco', attend_weights, value_single_float)
    outside_mask = jnp.einsum('xod,odn->xon', query_single_float, rounded_output(carried_state)) * entering_state
    decayed_keys = rounded_output(key_single_float * leaving_state)
    state_update = jnp.einsum('czm,czd->zmd', decayed_keys, value_single_float)
    return (passing[:, None, None] * carried_state + state_update, (inside + outside_mask, carried_state))

def backward_block(grad_state, inputs):
    query_block, key_block, value_block, log_rates, starts, full_out, carried_state, grad_block = inputs
    weights, entering_state, leaving_state, passing = block_parts(log_rates, starts)
    query_single_float = query_block.astype(jnp.float32)
    key_single_float = key_block.astype(jnp.float32)
    value_single_float = value_block.astype(jnp.float32)
    factor = lax.rsqrt(lax.optimization_barrier(jnp.mean(full_out * full_out, axis=-1, keepdims=True)) + EPS)
    grad_float = grad_block.astype(jnp.float32)
    gradient_precise = rounded_output(factor * grad_float - factor * factor * factor * full_out * lax.optimization_barrier(jnp.mean(grad_float * full_out, axis=-1, keepdims=True)))
    attend_weights = rounded_output(jnp.einsum('thd,shd->hts', query_single_float, key_single_float) * weights)
    attend_gradient = rounded_output(jnp.einsum('thd,shd->hts', gradient_precise, value_single_float) * weights)
    state_reduced = rounded_output(carried_state)
    gradient_reduced = rounded_output(grad_state)
    query_gradient = jnp.einsum('cnr,rco->nco', attend_gradient, key_single_float) + jnp.einsum('njx,jcx->njc', gradient_precise, state_reduced) * entering_state
    key_gradient = jnp.einsum('eng,neu->geu', attend_gradient, query_single_float) + jnp.einsum('lxp,xtp->lxt', value_single_float, gradient_reduced) * leaving_state
    value_gradient = jnp.einsum('eng,neu->geu', attend_weights, gradient_precise) + jnp.einsum('wld,ldp->wlp', key_single_float, gradient_reduced) * leaving_state
    decayed_queries = rounded_output(query_single_float * entering_state)
    partial_state = jnp.einsum('zlj,zla->lja', decayed_queries, gradient_precise)
    new_grad = passing[:, None, None] * grad_state + partial_state
    return (new_grad, (query_gradient.astype(jnp.bfloat16), key_gradient.astype(jnp.bfloat16), value_gradient.astype(jnp.bfloat16)))

def reference(query_in, key_in, value_in, log_decay, doc_start, out_grad):
    blocks = PACKED_TOKENS // BLOCK

    def split(flat_rows):
        return flat_rows.reshape(blocks, BLOCK, HEAD_TOTAL, DH)
    log_rates = jnp.moveaxis(log_decay.reshape(HEAD_TOTAL, blocks, BLOCK), 1, 0)
    starts = doc_start.reshape(blocks, BLOCK)
    inputs = (split(query_in), split(key_in), split(value_in), log_rates, starts)
    zero_state = jnp.zeros((HEAD_TOTAL, DH, DH), jnp.float32)
    final_state, (full_out, carried_state) = lax.scan(forward_block, zero_state, inputs)
    factor = lax.rsqrt(lax.optimization_barrier(jnp.mean(full_out * full_out, axis=-1, keepdims=True)) + EPS)
    normed = (full_out * factor).astype(jnp.bfloat16).reshape(PACKED_TOKENS, HEAD_TOTAL * DH)
    final_grad, (query_gradient, key_gradient, value_gradient) = lax.scan(backward_block, zero_state, inputs + (full_out, carried_state, split(out_grad)), reverse=True)
    return (normed, query_gradient.reshape(PACKED_TOKENS, HEAD_TOTAL * DH), key_gradient.reshape(PACKED_TOKENS, HEAD_TOTAL * DH), value_gradient.reshape(PACKED_TOKENS, HEAD_TOTAL * DH))
```

```python
import functools

import jax
import jax.numpy as jnp
from jax import lax
from jax.experimental import pallas as pl
from jax.experimental.pallas import tpu as pltpu
from jax.sharding import PartitionSpec as P

C = 128
EPS = 1e-06
NEG = -1e30
GROUPS = 2
F32 = jnp.float32
BF16 = jnp.bfloat16
VMEM_LIMIT = 48 * 1024 * 1024


def dot(a, b):
    return lax.dot_general(a, b, (((1,), (0,)), ((), ())), preferred_element_type=F32)


def dot_t(a, b):
    return lax.dot_general(a, b, (((1,), (1,)), ((), ())), preferred_element_type=F32)


def t_dot(a, b):
    return lax.dot_general(a, b, (((0,), (0,)), ((), ())), preferred_element_type=F32)


def exact_dot(a, b):
    return lax.dot_general(
        a, b, (((1,), (0,)), ((), ())), precision=lax.Precision.HIGHEST, preferred_element_type=F32
    )


def columns(row):
    return jnp.broadcast_to(row, (C, C)).T


def prepare_kernel(chunks, decay_ref, start_ref, run_ref, table_ref, gain_ref, weight_bias_ref, enter_bias_ref, leave_bias_ref):
    heads = decay_ref.shape[0]
    at_row = lax.broadcasted_iota(jnp.int32, (C, C), 0)
    at_lane = lax.broadcasted_iota(jnp.int32, (C, C), 1)
    upper = jnp.where(at_row <= at_lane, 1.0, 0.0).astype(F32)
    ones = jnp.ones((C, C), F32)
    gain = jnp.ones((heads, C), F32)
    for j in range(chunks):
        span = pl.ds(j * C, C)
        decay = decay_ref[:, span]
        run = exact_dot(decay, upper)
        last = exact_dot(decay, ones)
        starts = jnp.broadcast_to(start_ref[:, span].astype(F32), (8, C))
        docs = exact_dot(starts, upper)[:1]
        docs_last = exact_dot(starts, ones)[:1]
        passing = jnp.where(docs_last == 0.0, jnp.exp(last), 0.0)
        gain = gain * passing
        run_ref[:, 0, span] = run
        table_ref[:, j, :] = passing
        table_ref[:, chunks + j, :] = last
        docs_column = columns(docs)
        weight_bias_ref[span, :] = jnp.where((docs_column == docs) & (at_lane <= at_row), 0.0, NEG)
        enter_bias_ref[span, :] = jnp.where(docs_column == 0.0, 0.0, NEG)
        leave_bias_ref[span, :] = jnp.where(docs_column == docs_last, 0.0, NEG)
    gain_ref[...] = gain


def state_kernel(chunks, quarter, core_ref, k_ref, v_ref, run_ref, table_ref, leave_bias_ref, prefix_ref, mine_ref, other_ref):
    p = pl.program_id(0)
    total = None
    for j in range(chunks):
        span = pl.ds(j * C, C)
        run = columns(run_ref[0, :, span])
        leave = jnp.exp(table_ref[0, chunks + j : chunks + j + 1, :] - run + leave_bias_ref[span, :])
        kd = (k_ref[span, :].astype(F32) * leave).astype(BF16)
        update = t_dot(kd, v_ref[span, :])
        total = update if total is None else table_ref[0, j : j + 1, :] * total + update
        if j < chunks - 1:
            prefix_ref[0, j] = total

    @pl.when(p < quarter)
    def _():
        mine_ref[0] = total

    @pl.when(p >= quarter)
    def _():
        other_ref[0] = total


def forward_kernel(
    chunks, quarter, core_ref, q_ref, k_ref, v_ref, og_ref, run_ref, table_ref, weight_bias_ref, enter_bias_ref,
    prefix_ref, keep_ref, back_ref, *rest
):
    normed_ref, grad_ref, suffix_ref, mine_ref, other_ref = rest[-5:]
    p = pl.program_id(0)
    incoming = jnp.where(p < quarter, keep_ref[0], back_ref[0])
    gain = None
    parts = []
    for j in range(chunks):
        span = pl.ds(j * C, C)
        row = run_ref[0, :, span]
        run = columns(row)
        weights = jnp.exp(run - row + weight_bias_ref[span, :])
        enter = jnp.exp(run + enter_bias_ref[span, :])
        q, k, v = q_ref[span, :], k_ref[span, :], v_ref[span, :]
        attend = (dot_t(q, k) * weights).astype(BF16)
        state = incoming if j == 0 else gain * incoming + prefix_ref[0, j - 1]
        passing = table_ref[0, j : j + 1, :]
        gain = passing if gain is None else gain * passing
        out = dot(attend, v) + enter * dot(q, state.astype(BF16))
        factor = lax.rsqrt(jnp.mean(out * out, axis=-1, keepdims=True) + EPS)
        normed = out * factor
        normed_ref[span, :] = normed.astype(BF16)
        og = og_ref[span, :].astype(F32)
        along = jnp.mean(og * out, axis=-1, keepdims=True)
        grad = (factor * og - (factor * factor * factor * along) * out).astype(BF16)
        grad_ref[span, :] = grad
        qd = (q.astype(F32) * enter).astype(BF16)
        parts.append(t_dot(qd, grad))
    total = parts[-1]
    for j in range(chunks - 2, -1, -1):
        suffix_ref[0, j] = total
        total = table_ref[0, j : j + 1, :] * total + parts[j]

    @pl.when(p < quarter)
    def _():
        mine_ref[0] = total

    @pl.when(p >= quarter)
    def _():
        other_ref[0] = total


def backward_kernel(
    chunks, quarter, core_ref, q_ref, k_ref, v_ref, g_ref, run_ref, table_ref, weight_bias_ref, enter_bias_ref,
    leave_bias_ref, prefix_ref, suffix_ref, keep_ref, back_ref, gkeep_ref, gback_ref, *rest
):
    dq_ref, dk_ref, dv_ref = rest[-3:]
    p = pl.program_id(0)
    incoming = jnp.where(p < quarter, keep_ref[0], back_ref[0])
    outgoing = jnp.where(p < quarter, gkeep_ref[0], gback_ref[0])
    states = []
    gain = None
    for j in range(chunks):
        states.append((incoming if j == 0 else gain * incoming + prefix_ref[0, j - 1]).astype(BF16))
        passing = table_ref[0, j : j + 1, :]
        gain = passing if gain is None else gain * passing
    gain = None
    for j in range(chunks - 1, -1, -1):
        span = pl.ds(j * C, C)
        row = run_ref[0, :, span]
        run = columns(row)
        weights = jnp.exp(run - row + weight_bias_ref[span, :])
        enter = jnp.exp(run + enter_bias_ref[span, :])
        leave = jnp.exp(table_ref[0, chunks + j : chunks + j + 1, :] - run + leave_bias_ref[span, :])
        q, k, v, g = q_ref[span, :], k_ref[span, :], v_ref[span, :], g_ref[span, :]
        attend = (dot_t(q, k) * weights).astype(BF16)
        dattend = (dot_t(g, v) * weights).astype(BF16)
        gstate = outgoing if j == chunks - 1 else gain * outgoing + suffix_ref[0, j]
        passing = table_ref[0, j : j + 1, :]
        gain = passing if gain is None else gain * passing
        gstate = gstate.astype(BF16)
        dq = dot(dattend, k) + enter * dot_t(g, states[j])
        dk = t_dot(dattend, q) + leave * dot_t(v, gstate)
        dv = t_dot(attend, g) + leave * dot(k, gstate)
        dq_ref[span, :] = dq.astype(BF16)
        dk_ref[span, :] = dk.astype(BF16)
        dv_ref[span, :] = dv.astype(BF16)


def local(query_in, key_in, value_in, log_decay, doc_start, out_grad):
    length, width = query_in.shape
    heads = log_decay.shape[0]
    dh = width // heads
    chunks = length // C
    groups = GROUPS
    size = heads // groups
    quarter = size // 2
    shards = lax.axis_size("seq")
    core = lax.axis_index("ctx")
    first = core == 0
    core_arg = core.astype(jnp.int32).reshape(1)
    swap = [(0, 1), (1, 0)]
    shape = jax.ShapeDtypeStruct

    run, table, gain, weight_bias, enter_bias, leave_bias = pl.pallas_call(
        functools.partial(prepare_kernel, chunks),
        out_shape=(
            shape((heads, 1, length), F32),
            shape((heads, 2 * chunks, C), F32),
            shape((heads, C), F32),
            shape((length, C), F32),
            shape((length, C), F32),
            shape((length, C), F32),
        ),
        name="prepare",
    )(log_decay, doc_start.reshape(1, length))
    gain_other = lax.ppermute(gain, "ctx", swap)
    gain0 = jnp.where(first, gain, gain_other)
    gain1 = jnp.where(first, gain_other, gain)

    def specs(group):
        def head(p, core_ref):
            return group * size + lax.rem(p + core_ref[0] * quarter, size)

        return dict(
            rows=pl.BlockSpec((length, dh), lambda p, c: (0, head(p, c))),
            run=pl.BlockSpec((1, 1, length), lambda p, c: (head(p, c), 0, 0)),
            table=pl.BlockSpec((1, 2 * chunks, C), lambda p, c: (head(p, c), 0, 0)),
            bias=pl.BlockSpec((length, C), lambda p, c: (0, 0)),
            states=pl.BlockSpec((1, chunks - 1, dh, dh), lambda p, c: (p, 0, 0, 0)),
            mine=pl.BlockSpec((1, dh, dh), lambda p, c: (jnp.minimum(p, quarter - 1), 0, 0)),
            other=pl.BlockSpec((1, dh, dh), lambda p, c: (jnp.maximum(p - quarter, 0), 0, 0)),
            any=pl.BlockSpec(memory_space=pl.ANY),
        )

    states_shape = shape((size, chunks - 1, dh, dh), F32)
    part_shape = shape((quarter, dh, dh), F32)
    rows_shape = shape((length, width), BF16)

    def call(kernel, group, in_names, out_names, out_shapes, args, name, products, reads, aliases=()):
        table = specs(group)
        extra = [a for a in aliases if a is not None]
        return pl.pallas_call(
            functools.partial(kernel, chunks, quarter),
            grid_spec=pltpu.PrefetchScalarGridSpec(
                num_scalar_prefetch=1,
                grid=(size,),
                in_specs=[table[n] for n in in_names] + [table["any"]] * len(extra),
                out_specs=[table[n] for n in out_names],
            ),
            out_shape=out_shapes,
            input_output_aliases={1 + len(in_names) + i: i for i in range(len(extra))},
            compiler_params=pltpu.CompilerParams(
                dimension_semantics=("arbitrary",), vmem_limit_bytes=VMEM_LIMIT
            ),
            cost_estimate=pl.CostEstimate(
                flops=products * size * 2 * length * C * dh,
                bytes_accessed=reads * size * length * dh * 2,
                transcendentals=size * length * C,
            ),
            name=name,
        )(core_arg, *args, *extra)

    def pick(array, group):
        start = group * size + core * quarter
        return lax.dynamic_slice_in_dim(array, start, quarter, 0)[:, None, :]

    def carry(group, mine, other, backward):
        g0, g1 = pick(gain0, group), pick(gain1, group)
        got = lax.ppermute(other, "ctx", swap)
        zero = jnp.where(first, mine, got)
        one = jnp.where(first, got, mine)
        both = g0 * g1
        if backward:
            total = g0 * one + zero
            order = [(k, k - 1) for k in range(shards - 1, 0, -1)]
        else:
            total = g1 * zero + one
            order = [(k, k + 1) for k in range(shards - 1)]
        state = None
        for hop in order:
            sent = total if state is None else both * state + total
            landed = lax.ppermute(sent, "seq", [hop])
            state = landed if state is None else state + landed
        if backward:
            inner = g1 * state + one
            keep, send = jnp.where(first, inner, state), jnp.where(first, state, inner)
        else:
            inner = g0 * state + zero
            keep, send = jnp.where(first, state, inner), jnp.where(first, inner, state)
        return keep, lax.ppermute(send, "ctx", swap)

    prefixes, updates = [], []
    for group in range(groups):
        prefix, mine, other = call(
            state_kernel, group,
            ["rows", "rows", "run", "table", "bias"],
            ["states", "mine", "other"],
            (states_shape, part_shape, part_shape),
            (key_in, value_in, run, table, leave_bias),
            "state", 1, 4,
        )
        prefixes.append(prefix)
        updates.append((mine, other))
    incoming = [carry(group, *updates[group], False) for group in range(groups)]

    normed = grad = None
    suffixes, outgoing = [], []
    for group in range(groups):
        normed, grad_new, suffix, mine, other = call(
            forward_kernel, group,
            ["rows"] * 4 + ["run", "table", "bias", "bias", "states", "mine", "other"],
            ["rows", "rows", "states", "mine", "other"],
            (rows_shape, rows_shape, states_shape, part_shape, part_shape),
            (query_in, key_in, value_in, out_grad, run, table, weight_bias, enter_bias, prefixes[group], *incoming[group]),
            "forward", 4, 8,
            aliases=(normed,),
        )
        grad = grad_new
        suffixes.append((grad, suffix))
        outgoing.append(carry(group, mine, other, True))

    grads = (None, None, None)
    for group in range(groups):
        grad, suffix = suffixes[group]
        grads = call(
            backward_kernel, group,
            ["rows"] * 4 + ["run", "table", "bias", "bias", "bias", "states", "states", "mine", "other", "mine", "other"],
            ["rows", "rows", "rows"],
            (rows_shape, rows_shape, rows_shape),
            (
                query_in, key_in, value_in, grad, run, table, weight_bias, enter_bias, leave_bias,
                prefixes[group], suffix, *incoming[group], *outgoing[group],
            ),
            "backward", 8, 10,
            aliases=grads,
        )
    return (normed, *grads)


def solution(mesh):
    rows = P(("groups", "seq", "ctx"), "tensor")
    return jax.shard_map(
        local,
        mesh=mesh,
        in_specs=(rows, rows, rows, P("tensor", ("groups", "seq", "ctx")), P(("groups", "seq", "ctx")), rows),
        out_specs=(rows, rows, rows, rows),
        check_vma=False,
    )
```

```python
import functools

import jax
import jax.numpy as jnp
from jax import lax
from jax.experimental import pallas as pl
from jax.experimental.pallas import tpu as pltpu
from jax.sharding import PartitionSpec as P

C = 128
EPS = 1e-06
NEG = -1e30
GROUPS = 2
F32 = jnp.float32
BF16 = jnp.bfloat16
VMEM_LIMIT = 32 * 1024 * 1024


def dot(a, b):
    return lax.dot_general(a, b, (((1,), (0,)), ((), ())), preferred_element_type=F32)


def dot_t(a, b):
    return lax.dot_general(a, b, (((1,), (1,)), ((), ())), preferred_element_type=F32)


def t_dot(a, b):
    return lax.dot_general(a, b, (((0,), (0,)), ((), ())), preferred_element_type=F32)


def exact_dot(a, b):
    return lax.dot_general(
        a, b, (((1,), (0,)), ((), ())), precision=lax.Precision.HIGHEST, preferred_element_type=F32
    )


def columns(row):
    return jnp.broadcast_to(row, (C, C)).T


def prepare_kernel(chunks, decay_ref, start_ref, run_ref, table_ref, gain_ref, weight_bias_ref, enter_bias_ref, leave_bias_ref):
    heads = decay_ref.shape[0]
    at_row = lax.broadcasted_iota(jnp.int32, (C, C), 0)
    at_lane = lax.broadcasted_iota(jnp.int32, (C, C), 1)
    upper = jnp.where(at_row <= at_lane, 1.0, 0.0).astype(F32)
    ones = jnp.ones((C, C), F32)
    gain = jnp.ones((heads, C), F32)
    for j in range(chunks):
        span = pl.ds(j * C, C)
        decay = decay_ref[:, span]
        run = exact_dot(decay, upper)
        last = exact_dot(decay, ones)
        starts = jnp.broadcast_to(start_ref[:, span].astype(F32), (8, C))
        docs = exact_dot(starts, upper)[:1]
        docs_last = exact_dot(starts, ones)[:1]
        passing = jnp.where(docs_last == 0.0, jnp.exp(last), 0.0)
        gain = gain * passing
        run_ref[:, 0, span] = run
        table_ref[:, j, :] = passing
        table_ref[:, chunks + j, :] = last
        docs_column = columns(docs)
        weight_bias_ref[span, :] = jnp.where((docs_column == docs) & (at_lane <= at_row), 0.0, NEG)
        enter_bias_ref[span, :] = jnp.where(docs_column == 0.0, 0.0, NEG)
        leave_bias_ref[span, :] = jnp.where(docs_column == docs_last, 0.0, NEG)
    gain_ref[...] = gain


def state_kernel(chunks, quarter, core_ref, k_ref, v_ref, run_ref, table_ref, leave_bias_ref, prefix_ref, mine_ref, other_ref):
    p = pl.program_id(0)
    spans = [pl.ds(j * C, C) for j in range(chunks)]
    runs = [columns(run_ref[0, :, span]) for span in spans]
    leaves = [
        jnp.exp(table_ref[0, chunks + j : chunks + j + 1, :] - runs[j] + leave_bias_ref[spans[j], :])
        for j in range(chunks)
    ]
    kds = [(k_ref[spans[j], :].astype(F32) * leaves[j]).astype(BF16) for j in range(chunks)]
    updates = [t_dot(kds[j], v_ref[spans[j], :]) for j in range(chunks)]
    total = None
    for j in range(chunks):
        total = updates[j] if total is None else table_ref[0, j : j + 1, :] * total + updates[j]
        if j < chunks - 1:
            prefix_ref[0, j] = total

    @pl.when(p < quarter)
    def _():
        mine_ref[0] = total

    @pl.when(p >= quarter)
    def _():
        other_ref[0] = total


def entering_states(chunks, incoming, table_ref, prefix_ref):
    states, gain = [], None
    for j in range(chunks):
        states.append((incoming if j == 0 else gain * incoming + prefix_ref[0, j - 1]).astype(BF16))
        passing = table_ref[0, j : j + 1, :]
        gain = passing if gain is None else gain * passing
    return states


def forward_kernel(
    chunks, quarter, core_ref, q_ref, k_ref, v_ref, og_ref, run_ref, table_ref, weight_bias_ref, enter_bias_ref,
    prefix_ref, keep_ref, back_ref, *rest
):
    normed_ref, grad_ref, suffix_ref, mine_ref, other_ref = rest[-5:]
    p = pl.program_id(0)
    each = range(chunks)
    spans = [pl.ds(j * C, C) for j in each]
    incoming = jnp.where(p < quarter, keep_ref[0], back_ref[0])
    states = entering_states(chunks, incoming, table_ref, prefix_ref)
    q = [q_ref[span, :] for span in spans]
    scores = [dot_t(q[j], k_ref[spans[j], :]) for j in each]
    outside = [dot(q[j], states[j]) for j in each]
    rows = [run_ref[0, :, span] for span in spans]
    runs = [columns(row) for row in rows]
    attends = [
        (scores[j] * jnp.exp(runs[j] - rows[j] + weight_bias_ref[spans[j], :])).astype(BF16) for j in each
    ]
    enters = [jnp.exp(runs[j] + enter_bias_ref[spans[j], :]) for j in each]
    qds = [(q[j].astype(F32) * enters[j]).astype(BF16) for j in each]
    outs = [dot(attends[j], v_ref[spans[j], :]) + enters[j] * outside[j] for j in each]
    squares = [jnp.mean(outs[j] * outs[j], axis=-1, keepdims=True) for j in each]
    ogs = [og_ref[span, :].astype(F32) for span in spans]
    alongs = [jnp.mean(ogs[j] * outs[j], axis=-1, keepdims=True) for j in each]
    factors = [lax.rsqrt(square + EPS) for square in squares]
    grads = []
    for j in each:
        normed = outs[j] * factors[j]
        normed_ref[spans[j], :] = normed.astype(BF16)
        grad = (factors[j] * (ogs[j] - (factors[j] * alongs[j]) * normed)).astype(BF16)
        grad_ref[spans[j], :] = grad
        grads.append(grad)
    parts = [t_dot(qds[j], grads[j]) for j in each]
    total = parts[-1]
    for j in range(chunks - 2, -1, -1):
        suffix_ref[0, j] = total
        total = table_ref[0, j : j + 1, :] * total + parts[j]

    @pl.when(p < quarter)
    def _():
        mine_ref[0] = total

    @pl.when(p >= quarter)
    def _():
        other_ref[0] = total


def backward_kernel(
    chunks, quarter, core_ref, q_ref, k_ref, v_ref, g_ref, run_ref, table_ref, weight_bias_ref, enter_bias_ref,
    leave_bias_ref, prefix_ref, suffix_ref, keep_ref, back_ref, gkeep_ref, gback_ref, *rest
):
    dq_ref, dk_ref, dv_ref = rest[-3:]
    p = pl.program_id(0)
    each = range(chunks)
    spans = [pl.ds(j * C, C) for j in each]
    incoming = jnp.where(p < quarter, keep_ref[0], back_ref[0])
    outgoing = jnp.where(p < quarter, gkeep_ref[0], gback_ref[0])
    states = entering_states(chunks, incoming, table_ref, prefix_ref)
    gstates, gain = [None] * chunks, None
    for j in range(chunks - 1, -1, -1):
        gstates[j] = (outgoing if j == chunks - 1 else gain * outgoing + suffix_ref[0, j]).astype(BF16)
        passing = table_ref[0, j : j + 1, :]
        gain = passing if gain is None else gain * passing
    q, k, v, g = ([ref[span, :] for span in spans] for ref in (q_ref, k_ref, v_ref, g_ref))
    scores = [dot_t(q[j], k[j]) for j in each]
    dscores = [dot_t(g[j], v[j]) for j in each]
    rows = [run_ref[0, :, span] for span in spans]
    runs = [columns(row) for row in rows]
    weights = [jnp.exp(runs[j] - rows[j] + weight_bias_ref[spans[j], :]) for j in each]
    attends = [(scores[j] * weights[j]).astype(BF16) for j in each]
    dattends = [(dscores[j] * weights[j]).astype(BF16) for j in each]
    enters = [jnp.exp(runs[j] + enter_bias_ref[spans[j], :]) for j in each]
    leaves = [
        jnp.exp(table_ref[0, chunks + j : chunks + j + 1, :] - runs[j] + leave_bias_ref[spans[j], :]) for j in each
    ]
    for j in each:
        dq_ref[spans[j], :] = (dot(dattends[j], k[j]) + enters[j] * dot_t(g[j], states[j])).astype(BF16)
    for j in each:
        dk_ref[spans[j], :] = (t_dot(dattends[j], q[j]) + leaves[j] * dot_t(v[j], gstates[j])).astype(BF16)
    for j in each:
        dv_ref[spans[j], :] = (t_dot(attends[j], g[j]) + leaves[j] * dot(k[j], gstates[j])).astype(BF16)


def block_specs(group, size, quarter, chunks, length, dh):
    def head(p, core_ref):
        return group * size + lax.rem(p + core_ref[0] * quarter, size)

    return dict(
        rows=pl.BlockSpec((length, dh), lambda p, c: (0, head(p, c))),
        run=pl.BlockSpec((1, 1, length), lambda p, c: (head(p, c), 0, 0)),
        table=pl.BlockSpec((1, 2 * chunks, C), lambda p, c: (head(p, c), 0, 0)),
        bias=pl.BlockSpec((length, C), lambda p, c: (0, 0)),
        states=pl.BlockSpec((1, chunks - 1, dh, dh), lambda p, c: (p, 0, 0, 0)),
        mine=pl.BlockSpec((1, dh, dh), lambda p, c: (jnp.minimum(p, quarter - 1), 0, 0)),
        other=pl.BlockSpec((1, dh, dh), lambda p, c: (jnp.maximum(p - quarter, 0), 0, 0)),
        any=pl.BlockSpec(memory_space=pl.ANY),
    )


def call_heads(dims, core_arg, kernel, group, in_names, out_names, out_shapes, args, name, products, reads, aliases=()):
    size, quarter, chunks, length, dh = dims
    table = block_specs(group, *dims)
    extra = [a for a in aliases if a is not None]
    return pl.pallas_call(
        functools.partial(kernel, chunks, quarter),
        grid_spec=pltpu.PrefetchScalarGridSpec(
            num_scalar_prefetch=1,
            grid=(size,),
            in_specs=[table[n] for n in in_names] + [table["any"]] * len(extra),
            out_specs=[table[n] for n in out_names],
        ),
        out_shape=out_shapes,
        input_output_aliases={1 + len(in_names) + i: i for i in range(len(extra))},
        compiler_params=pltpu.CompilerParams(
            dimension_semantics=("arbitrary",), vmem_limit_bytes=VMEM_LIMIT
        ),
        cost_estimate=pl.CostEstimate(
            flops=products * size * 2 * length * C * dh,
            bytes_accessed=reads * size * length * dh * 2,
            transcendentals=size * length * C,
        ),
        name=name,
    )(core_arg, *args, *extra)


def local(query_in, key_in, value_in, log_decay, doc_start, out_grad):
    length, width = query_in.shape
    heads = log_decay.shape[0]
    dh = width // heads
    chunks = length // C
    groups = GROUPS
    size = heads // groups
    quarter = size // 2
    shards = lax.axis_size("seq")
    core = lax.axis_index("ctx")
    first = core == 0
    core_arg = core.astype(jnp.int32).reshape(1)
    swap = [(0, 1), (1, 0)]
    shape = jax.ShapeDtypeStruct

    run, table, gain, weight_bias, enter_bias, leave_bias = pl.pallas_call(
        functools.partial(prepare_kernel, chunks),
        out_shape=(
            shape((heads, 1, length), F32),
            shape((heads, 2 * chunks, C), F32),
            shape((heads, C), F32),
            shape((length, C), F32),
            shape((length, C), F32),
            shape((length, C), F32),
        ),
        name="prepare",
    )(log_decay, doc_start.reshape(1, length))
    gain_other = lax.ppermute(gain, "ctx", swap)
    gain0 = jnp.where(first, gain, gain_other)
    gain1 = jnp.where(first, gain_other, gain)

    states_shape = shape((size, chunks - 1, dh, dh), F32)
    part_shape = shape((quarter, dh, dh), F32)
    rows_shape = shape((length, width), BF16)

    call = functools.partial(call_heads, (size, quarter, chunks, length, dh), core_arg)

    def pick(array, group):
        start = group * size + core * quarter
        return lax.dynamic_slice_in_dim(array, start, quarter, 0)[:, None, :]

    def carry(group, mine, other, backward):
        g0, g1 = pick(gain0, group), pick(gain1, group)
        got = lax.ppermute(other, "ctx", swap)
        zero = jnp.where(first, mine, got)
        one = jnp.where(first, got, mine)
        both = g0 * g1
        if backward:
            total = g0 * one + zero
            order = [(k, k - 1) for k in range(shards - 1, 0, -1)]
        else:
            total = g1 * zero + one
            order = [(k, k + 1) for k in range(shards - 1)]
        state = None
        for hop in order:
            sent = total if state is None else both * state + total
            landed = lax.ppermute(sent, "seq", [hop])
            state = landed if state is None else state + landed
        if backward:
            inner = g1 * state + one
            keep, send = jnp.where(first, inner, state), jnp.where(first, state, inner)
        else:
            inner = g0 * state + zero
            keep, send = jnp.where(first, state, inner), jnp.where(first, inner, state)
        return keep, lax.ppermute(send, "ctx", swap)

    prefixes, updates = [], []
    for group in range(groups):
        prefix, mine, other = call(
            state_kernel, group,
            ["rows", "rows", "run", "table", "bias"],
            ["states", "mine", "other"],
            (states_shape, part_shape, part_shape),
            (key_in, value_in, run, table, leave_bias),
            "state", 1, 4,
        )
        prefixes.append(prefix)
        updates.append((mine, other))
    incoming = [carry(group, *updates[group], False) for group in range(groups)]

    normed = grad = None
    suffixes, outgoing = [], []
    for group in range(groups):
        normed, grad_new, suffix, mine, other = call(
            forward_kernel, group,
            ["rows"] * 4 + ["run", "table", "bias", "bias", "states", "mine", "other"],
            ["rows", "rows", "states", "mine", "other"],
            (rows_shape, rows_shape, states_shape, part_shape, part_shape),
            (query_in, key_in, value_in, out_grad, run, table, weight_bias, enter_bias, prefixes[group], *incoming[group]),
            "forward", 4, 8,
            aliases=(normed,),
        )
        grad = grad_new
        suffixes.append((grad, suffix))
        outgoing.append(carry(group, mine, other, True))

    grads = (None, None, None)
    for group in range(groups):
        grad, suffix = suffixes[group]
        grads = call(
            backward_kernel, group,
            ["rows"] * 4 + ["run", "table", "bias", "bias", "bias", "states", "states", "mine", "other", "mine", "other"],
            ["rows", "rows", "rows"],
            (rows_shape, rows_shape, rows_shape),
            (
                query_in, key_in, value_in, grad, run, table, weight_bias, enter_bias, leave_bias,
                prefixes[group], suffix, *incoming[group], *outgoing[group],
            ),
            "backward", 8, 10,
            aliases=grads,
        )
    return (normed, *grads)


def solution(mesh):
    rows = P(("groups", "seq", "ctx"), "tensor")
    return jax.shard_map(
        local,
        mesh=mesh,
        in_specs=(rows, rows, rows, P("tensor", ("groups", "seq", "ctx")), P(("groups", "seq", "ctx")), rows),
        out_specs=(rows, rows, rows, rows),
        check_vma=False,
    )
```

```python
import functools

import jax
import jax.numpy as jnp
from jax import lax
from jax.experimental import pallas as pl
from jax.experimental.pallas import tpu as pltpu
from jax.sharding import PartitionSpec as P

C = 128
EPS = 1e-06
NEG = -1e30
GROUPS = 2
PER_STEP = 2
F32 = jnp.float32
BF16 = jnp.bfloat16
VMEM_LIMIT = 32 * 1024 * 1024
VMEM_ALL = 62 * 1024 * 1024


def dot(a, b):
    return lax.dot_general(a, b, (((1,), (0,)), ((), ())), preferred_element_type=F32)


def dot_t(a, b):
    return lax.dot_general(a, b, (((1,), (1,)), ((), ())), preferred_element_type=F32)


def t_dot(a, b):
    return lax.dot_general(a, b, (((0,), (0,)), ((), ())), preferred_element_type=F32)


def exact_dot(a, b):
    return lax.dot_general(
        a, b, (((1,), (0,)), ((), ())), precision=lax.Precision.HIGHEST, preferred_element_type=F32
    )


def columns(row):
    return jnp.broadcast_to(row, (C, C)).T


def fill_tables(chunks, decay_ref, start_ref, run_ref, table_ref, gain_ref, weight_bias_ref, enter_bias_ref, leave_bias_ref):
    heads = decay_ref.shape[0]
    at_row = lax.broadcasted_iota(jnp.int32, (C, C), 0)
    at_lane = lax.broadcasted_iota(jnp.int32, (C, C), 1)
    upper = jnp.where(at_row <= at_lane, 1.0, 0.0).astype(F32)
    sums = jnp.concatenate([upper, jnp.ones((C, C), F32)], axis=1)
    gain = jnp.ones((heads, C), F32)
    each = range(chunks)
    spans = [pl.ds(j * C, C) for j in each]
    runs = [exact_dot(decay_ref[:, span], sums) for span in spans]
    starts = jnp.concatenate([start_ref[:, span].astype(F32) for span in spans] * (8 // chunks), axis=0)
    docs_all = dot(starts.astype(BF16), sums.astype(BF16))
    for j in each:
        span = spans[j]
        last = runs[j][:, C:]
        docs, docs_last = docs_all[j : j + 1, :C], docs_all[j : j + 1, C:]
        passing = jnp.where(docs_last == 0.0, jnp.exp(last), 0.0)
        gain = gain * passing
        run_ref[:, 0, span] = runs[j][:, :C]
        table_ref[:, j, :] = passing
        table_ref[:, chunks + j, :] = last
        docs_column = columns(docs)
        weight_bias_ref[span, :] = jnp.where((docs_column == docs) & (at_lane <= at_row), 0.0, NEG)
        enter_bias_ref[span, :] = jnp.where(docs_column == 0.0, 0.0, NEG)
        leave_bias_ref[span, :] = jnp.where(docs_column == docs_last, 0.0, NEG)
    gain_ref[...] = gain


def items_of(chunks, per_step):
    return [(i, j, pl.ds(j * C, C), pl.ds(i * C, C)) for i in range(per_step) for j in range(chunks)]


def split_store(dims, mine_ref, other_ref, totals):
    mine = lax.rem(pl.program_id(0), dims.steps) * dims.per_step < dims.quarter

    @pl.when(mine)
    def _():
        for i, total in enumerate(totals):
            mine_ref[i] = total

    @pl.when(jnp.logical_not(mine))
    def _():
        for i, total in enumerate(totals):
            other_ref[i] = total


def split_load(dims, mine_ref, other_ref):
    mine = pl.program_id(0) * dims.per_step < dims.quarter
    return [jnp.where(mine, mine_ref[i], other_ref[i]) for i in range(dims.per_step)]


def state_body(dims, heads_at, k_ref, v_ref, run_ref, table_ref, leave_bias_ref, prefix_ref, mine_ref, other_ref):
    chunks = dims.chunks
    items = items_of(chunks, dims.per_step)
    runs = [columns(run_ref[heads_at + i, :, rows]) for i, j, rows, cols in items]
    leaves = [
        jnp.exp(table_ref[heads_at + i, pl.ds(chunks + j, 1), :] - run + leave_bias_ref[rows, :])
        for run, (i, j, rows, cols) in zip(runs, items)
    ]
    kds = [(k_ref[rows, cols].astype(F32) * leave).astype(BF16) for leave, (i, j, rows, cols) in zip(leaves, items)]
    updates = [t_dot(kd, v_ref[rows, cols]) for kd, (i, j, rows, cols) in zip(kds, items)]
    totals = []
    for i in range(dims.per_step):
        total = None
        for j in range(chunks):
            update = updates[i * chunks + j]
            total = update if total is None else table_ref[heads_at + i, pl.ds(j, 1), :] * total + update
            if j < chunks - 1:
                prefix_ref[i, j] = total
        totals.append(total)
    split_store(dims, mine_ref, other_ref, totals)


def begin_kernel(
    dims, core_ref, decay_ref, start_ref, k_ref, v_ref,
    prefix_ref, mine_ref, other_ref, run_ref, table_ref, gain_ref, weight_bias_ref, enter_bias_ref, leave_bias_ref
):
    @pl.when(pl.program_id(0) == 0)
    def _():
        fill_tables(
            dims.chunks, decay_ref, start_ref, run_ref, table_ref, gain_ref, weight_bias_ref, enter_bias_ref,
            leave_bias_ref,
        )

    heads_at = dims.head(0, pl.program_id(0), core_ref) * dims.per_step
    state_body(dims, heads_at, k_ref, v_ref, run_ref, table_ref, leave_bias_ref, prefix_ref, mine_ref, other_ref)


def entering_states(chunks, i, incoming, table_ref, prefix_ref):
    states, gain = [], None
    for j in range(chunks):
        states.append((incoming if j == 0 else gain * incoming + prefix_ref[i, j - 1]).astype(BF16))
        passing = table_ref[i, j : j + 1, :]
        gain = passing if gain is None else gain * passing
    return states


def leaving_states(chunks, i, outgoing, table_ref, suffix_ref):
    states, gain = [None] * chunks, None
    for j in range(chunks - 1, -1, -1):
        states[j] = (outgoing if j == chunks - 1 else gain * outgoing + suffix_ref[i, j]).astype(BF16)
        passing = table_ref[i, j : j + 1, :]
        gain = passing if gain is None else gain * passing
    return states


def forward_kernel(
    dims, core_ref, q_ref, k_ref, v_ref, og_ref, run_ref, table_ref, weight_bias_ref, enter_bias_ref,
    prefix_ref, keep_ref, back_ref, *rest
):
    normed_ref, grad_ref, suffix_ref, mine_ref, other_ref = rest[-5:]
    chunks = dims.chunks
    items = items_of(chunks, dims.per_step)
    states = []
    for i, incoming in enumerate(split_load(dims, keep_ref, back_ref)):
        states += entering_states(chunks, i, incoming, table_ref, prefix_ref)
    q = [q_ref[rows, cols] for i, j, rows, cols in items]
    scores = [dot_t(a, k_ref[rows, cols]) for a, (i, j, rows, cols) in zip(q, items)]
    outside = [dot(a, b) for a, b in zip(q, states)]
    marks = [run_ref[i, :, rows] for i, j, rows, cols in items]
    runs = [columns(mark) for mark in marks]
    attends = [
        (score * jnp.exp(run - mark + weight_bias_ref[rows, :])).astype(BF16)
        for score, run, mark, (i, j, rows, cols) in zip(scores, runs, marks, items)
    ]
    enters = [jnp.exp(run + enter_bias_ref[rows, :]) for run, (i, j, rows, cols) in zip(runs, items)]
    qds = [(a.astype(F32) * enter).astype(BF16) for a, enter in zip(q, enters)]
    outs = [
        dot(attend, v_ref[rows, cols]) + enter * far
        for attend, enter, far, (i, j, rows, cols) in zip(attends, enters, outside, items)
    ]
    squares = [jnp.mean(out * out, axis=-1, keepdims=True) for out in outs]
    ogs = [og_ref[rows, cols].astype(F32) for i, j, rows, cols in items]
    alongs = [jnp.mean(og * out, axis=-1, keepdims=True) for og, out in zip(ogs, outs)]
    factors = [lax.rsqrt(square + EPS) for square in squares]
    grads = []
    for out, factor, og, along, (i, j, rows, cols) in zip(outs, factors, ogs, alongs, items):
        normed = out * factor
        normed_ref[rows, cols] = normed.astype(BF16)
        grad = (factor * (og - (factor * along) * normed)).astype(BF16)
        grad_ref[rows, cols] = grad
        grads.append(grad)
    parts = [t_dot(qd, grad) for qd, grad in zip(qds, grads)]
    totals = []
    for i in range(dims.per_step):
        total = parts[i * chunks + chunks - 1]
        for j in range(chunks - 2, -1, -1):
            suffix_ref[i, j] = total
            total = table_ref[i, j : j + 1, :] * total + parts[i * chunks + j]
        totals.append(total)
    split_store(dims, mine_ref, other_ref, totals)


def backward_kernel(
    dims, core_ref, q_ref, k_ref, v_ref, g_ref, run_ref, table_ref, weight_bias_ref, enter_bias_ref,
    leave_bias_ref, prefix_ref, suffix_ref, keep_ref, back_ref, gkeep_ref, gback_ref, *rest
):
    dq_ref, dk_ref, dv_ref = rest[-3:]
    chunks = dims.chunks
    items = items_of(chunks, dims.per_step)
    states, gstates = [], []
    for i, incoming in enumerate(split_load(dims, keep_ref, back_ref)):
        states += entering_states(chunks, i, incoming, table_ref, prefix_ref)
    for i, outgoing in enumerate(split_load(dims, gkeep_ref, gback_ref)):
        gstates += leaving_states(chunks, i, outgoing, table_ref, suffix_ref)
    q, k, v, g = ([ref[rows, cols] for i, j, rows, cols in items] for ref in (q_ref, k_ref, v_ref, g_ref))
    n = range(len(items))
    scores = [dot_t(q[x], k[x]) for x in n]
    dscores = [dot_t(g[x], v[x]) for x in n]
    marks = [run_ref[i, :, rows] for i, j, rows, cols in items]
    runs = [columns(mark) for mark in marks]
    weights = [jnp.exp(runs[x] - marks[x] + weight_bias_ref[items[x][2], :]) for x in n]
    attends = [(scores[x] * weights[x]).astype(BF16) for x in n]
    dattends = [(dscores[x] * weights[x]).astype(BF16) for x in n]
    enters = [jnp.exp(runs[x] + enter_bias_ref[items[x][2], :]) for x in n]
    leaves = [
        jnp.exp(table_ref[i, chunks + j : chunks + j + 1, :] - run + leave_bias_ref[rows, :])
        for run, (i, j, rows, cols) in zip(runs, items)
    ]
    for x, (i, j, rows, cols) in enumerate(items):
        dq_ref[rows, cols] = (dot(dattends[x], k[x]) + enters[x] * dot_t(g[x], states[x])).astype(BF16)
    for x, (i, j, rows, cols) in enumerate(items):
        dk_ref[rows, cols] = (t_dot(dattends[x], q[x]) + leaves[x] * dot_t(v[x], gstates[x])).astype(BF16)
    for x, (i, j, rows, cols) in enumerate(items):
        dv_ref[rows, cols] = (t_dot(attends[x], g[x]) + leaves[x] * dot(k[x], gstates[x])).astype(BF16)


def after(value, token):
    return value if token is None else lax.optimization_barrier((value, token))[0]


class Dims:
    def __init__(self, size, per_step, chunks, length, dh, heads):
        self.size, self.per_step, self.chunks = size, per_step, chunks
        self.length, self.dh, self.heads = length, dh, heads
        self.quarter = size // 2
        self.steps = size // per_step

    def head(self, group, p, core_ref):
        return (group + p // self.steps) * self.steps + lax.rem(p + core_ref[0] * (self.steps // 2), self.steps)

    def specs(self, group):
        n, halves = self.per_step, self.steps // 2
        length, dh, chunks = self.length, self.dh, self.chunks
        whole = lambda *shape: pl.BlockSpec(shape, lambda p, c: (0,) * len(shape))
        return dict(
            rows=pl.BlockSpec((length, n * dh), lambda p, c: (0, self.head(group, p, c))),
            run=pl.BlockSpec((n, 1, length), lambda p, c: (self.head(group, p, c), 0, 0)),
            table=pl.BlockSpec((n, 2 * chunks, C), lambda p, c: (self.head(group, p, c), 0, 0)),
            bias=whole(length, C),
            states=pl.BlockSpec((n, chunks - 1, dh, dh), lambda p, c: (p, 0, 0, 0)),
            prefix=pl.BlockSpec((n, chunks - 1, dh, dh), lambda p, c: (p + group * self.steps, 0, 0, 0)),
            mine=pl.BlockSpec((n, dh, dh), lambda p, c: (p // self.steps * halves + jnp.minimum(lax.rem(p, self.steps), halves - 1), 0, 0)),
            other=pl.BlockSpec((n, dh, dh), lambda p, c: (p // self.steps * halves + jnp.maximum(lax.rem(p, self.steps) - halves, 0), 0, 0)),
            decay=whole(self.heads, length),
            start=whole(1, length),
            all_run=whole(self.heads, 1, length),
            all_table=whole(self.heads, 2 * chunks, C),
            all_gain=whole(self.heads, C),
            any=pl.BlockSpec(memory_space=pl.ANY),
        )


def call_heads(dims, core_arg, kernel, group, in_names, out_names, out_shapes, args, name, products, reads, aliases=(), tokens=(), vmem=VMEM_LIMIT, steps=None):
    specs = dims.specs(group)
    extra = [a for a in aliases if a is not None]
    return pl.pallas_call(
        functools.partial(kernel, dims),
        grid_spec=pltpu.PrefetchScalarGridSpec(
            num_scalar_prefetch=1,
            grid=(steps or dims.steps,),
            in_specs=[specs[n] for n in in_names] + [specs["any"]] * (len(extra) + len(tokens)),
            out_specs=[specs[n] for n in out_names],
        ),
        out_shape=out_shapes,
        input_output_aliases={1 + len(in_names) + i: i for i in range(len(extra))},
        compiler_params=pltpu.CompilerParams(
            dimension_semantics=("arbitrary",), vmem_limit_bytes=vmem
        ),
        cost_estimate=pl.CostEstimate(
            flops=products * dims.size * 2 * dims.length * C * dims.dh,
            bytes_accessed=reads * dims.size * dims.length * dims.dh * 2,
            transcendentals=dims.size * dims.length * C,
        ),
        name=name,
    )(core_arg, *args, *extra, *tokens)


def local(query_in, key_in, value_in, log_decay, doc_start, out_grad):
    length, width = query_in.shape
    heads = log_decay.shape[0]
    dh = width // heads
    chunks = length // C
    groups = GROUPS
    size = heads // groups
    quarter = size // 2
    dims = Dims(size, PER_STEP, chunks, length, dh, heads)
    shards = lax.axis_size("seq")
    core = lax.axis_index("ctx")
    first = core == 0
    core_arg = core.astype(jnp.int32).reshape(1)
    swap = [(0, 1), (1, 0)]
    shape = jax.ShapeDtypeStruct
    states_shape = shape((size, chunks - 1, dh, dh), F32)
    part_shape = shape((quarter, dh, dh), F32)
    rows_shape = shape((length, width), BF16)
    bias_shape = shape((length, C), F32)
    call = functools.partial(call_heads, dims, core_arg)

    prefix, mines, others, run, table, gain, weight_bias, enter_bias, leave_bias = call(
        begin_kernel, 0,
        ["decay", "start", "rows", "rows"],
        ["states", "mine", "other", "all_run", "all_table", "all_gain", "bias", "bias", "bias"],
        (
            shape((heads, chunks - 1, dh, dh), F32), shape((heads // 2, dh, dh), F32), shape((heads // 2, dh, dh), F32),
            shape((heads, 1, length), F32), shape((heads, 2 * chunks, C), F32), shape((heads, C), F32),
            bias_shape, bias_shape, bias_shape,
        ),
        (log_decay, doc_start.reshape(1, length), key_in, value_in),
        "begin", 1, 4,
        vmem=VMEM_ALL, steps=groups * dims.steps,
    )
    gain_other = lax.ppermute(gain, "ctx", swap)
    gain0 = jnp.where(first, gain, gain_other)
    gain1 = jnp.where(first, gain_other, gain)

    def pick(array, group):
        start = group * size + core * quarter
        return lax.dynamic_slice_in_dim(array, start, quarter, 0)[:, None, :]

    class Carry:
        def __init__(self, group, mine, other, backward):
            self.backward = backward
            self.g0, self.g1 = pick(gain0, group), pick(gain1, group)
            self.both = self.g0 * self.g1
            self.mine, self.got = mine, lax.ppermute(other, "ctx", swap)
            if backward:
                self.hops = [(k, k - 1) for k in range(shards - 1, 0, -1)]
            else:
                self.hops = [(k, k + 1) for k in range(shards - 1)]
            self.landed = []

        def start(self, token=None):
            got = after(self.got, token)
            self.zero = jnp.where(first, self.mine, got)
            self.one = jnp.where(first, got, self.mine)
            if self.backward:
                self.total = self.g0 * self.one + self.zero
            else:
                self.total = self.g1 * self.zero + self.one

        def hop(self, index, token=None):
            if index == 0:
                self.start(token)
                self.sent = self.total
            else:
                self.settle(token)
                self.sent = self.both * self.state + self.total
            self.landed.append(lax.ppermute(self.sent, "seq", [self.hops[index]]))

        def settle(self, token=None):
            self.landed[-1] = after(self.landed[-1], token)
            self.state = sum(self.landed[1:], self.landed[0])

        def finish(self, token=None):
            self.settle(token)
            state = self.state
            if self.backward:
                inner = self.g1 * state + self.one
                keep, send = jnp.where(first, inner, state), jnp.where(first, state, inner)
            else:
                inner = self.g0 * state + self.zero
                keep, send = jnp.where(first, state, inner), jnp.where(first, inner, state)
            return keep, lax.ppermute(send, "ctx", swap)

    hops = range(shards - 1)
    carries = []
    for group in range(groups):
        part = slice(group * quarter, (group + 1) * quarter)
        carries.append(Carry(group, mines[part], others[part], False))
    token = None
    for index in hops:
        for carry in carries:
            carry.hop(index, token)
            token = carry.sent

    normed = None
    incoming, suffixes, backs = [], [], []
    for group in range(groups):
        incoming.append(carries[group].finish(token))
        normed, grad, suffix, mine, other = call(
            forward_kernel, group,
            ["rows"] * 4 + ["run", "table", "bias", "bias", "prefix", "mine", "other"],
            ["rows", "rows", "states", "mine", "other"],
            (rows_shape, rows_shape, states_shape, part_shape, part_shape),
            (query_in, key_in, value_in, out_grad, run, table, weight_bias, enter_bias, prefix, *incoming[group]),
            "forward", 4, 8,
            aliases=(normed,),
            tokens=[backs[-1].sent] if backs else [],
        )
        token = mine
        suffixes.append((grad, suffix))
        backs.append(Carry(group, mine, other, True))
        if group == 0:
            backs[0].hop(0)
    for index in hops:
        for place, back in enumerate(backs):
            ahead = index + 1 if place == 0 else index
            if ahead in hops:
                back.hop(ahead, token)
                token = back.sent

    grads = (None, None, None)
    for group in range(groups):
        grad, suffix = suffixes[group]
        outgoing = backs[group].finish(token)
        grads = call(
            backward_kernel, group,
            ["rows"] * 4 + ["run", "table", "bias", "bias", "bias", "prefix", "states", "mine", "other", "mine", "other"],
            ["rows", "rows", "rows"],
            (rows_shape, rows_shape, rows_shape),
            (
                query_in, key_in, value_in, grad, run, table, weight_bias, enter_bias, leave_bias,
                prefix, suffix, *incoming[group], *outgoing,
            ),
            "backward", 8, 10,
            aliases=grads,
        )
        token = grads[0]
    return (normed, *grads)


def solution(mesh):
    rows = P(("groups", "seq", "ctx"), "tensor")
    return jax.shard_map(
        local,
        mesh=mesh,
        in_specs=(rows, rows, rows, P("tensor", ("groups", "seq", "ctx")), P(("groups", "seq", "ctx")), rows),
        out_specs=(rows, rows, rows, rows),
        check_vma=False,
    )
```

```python
import functools

import jax
import jax.numpy as jnp
from jax import lax
from jax.experimental import pallas as pl
from jax.experimental.pallas import tpu as pltpu
from jax.sharding import PartitionSpec as P

C = 128
EPS = 1e-06
NEG = -1e30
GROUPS = 2
PER_STEP = 2
F32 = jnp.float32
BF16 = jnp.bfloat16
VMEM_LIMIT = 20 * 1024 * 1024


def dot(a, b):
    return lax.dot_general(a, b, (((1,), (0,)), ((), ())), preferred_element_type=F32)


def dot_t(a, b):
    return lax.dot_general(a, b, (((1,), (1,)), ((), ())), preferred_element_type=F32)


def t_dot(a, b):
    return lax.dot_general(a, b, (((0,), (0,)), ((), ())), preferred_element_type=F32)


def exact_dot(a, b):
    return lax.dot_general(
        a, b, (((1,), (0,)), ((), ())), precision=lax.Precision.HIGHEST, preferred_element_type=F32
    )


def columns(row):
    return jnp.broadcast_to(row, (C, C)).T


def fill_tables(chunks, decay_ref, start_ref, run_ref, table_ref, gain_ref, weight_bias_ref, enter_bias_ref, leave_bias_ref):
    heads = decay_ref.shape[0]
    at_row = lax.broadcasted_iota(jnp.int32, (C, C), 0)
    at_lane = lax.broadcasted_iota(jnp.int32, (C, C), 1)
    upper = jnp.where(at_row <= at_lane, 1.0, 0.0).astype(F32)
    sums = jnp.concatenate([upper, jnp.ones((C, C), F32)], axis=1)
    gain = jnp.ones((heads, C), F32)
    each = range(chunks)
    spans = [pl.ds(j * C, C) for j in each]
    runs = [exact_dot(decay_ref[:, span], sums) for span in spans]
    starts = jnp.concatenate([start_ref[:, span].astype(F32) for span in spans] * (8 // chunks), axis=0)
    docs_all = dot(starts.astype(BF16), sums.astype(BF16))
    for j in each:
        span = spans[j]
        last = runs[j][:, C:]
        docs, docs_last = docs_all[j : j + 1, :C], docs_all[j : j + 1, C:]
        passing = jnp.where(docs_last == 0.0, jnp.exp(last), 0.0)
        gain = gain * passing
        run_ref[:, 0, span] = runs[j][:, :C]
        table_ref[:, j, :] = passing
        table_ref[:, chunks + j, :] = last
        docs_column = columns(docs)
        weight_bias_ref[span, :] = jnp.where((docs_column == docs) & (at_lane <= at_row), 0.0, NEG)
        enter_bias_ref[span, :] = jnp.where(docs_column == 0.0, 0.0, NEG)
        leave_bias_ref[span, :] = jnp.where(docs_column == docs_last, 0.0, NEG)
    gain_ref[...] = gain


def items_of(chunks, per_step):
    return [(i, j, pl.ds(j * C, C), pl.ds(i * C, C)) for i in range(per_step) for j in range(chunks)]


def split_store(dims, mine_ref, other_ref, totals):
    mine = pl.program_id(0) * dims.per_step < dims.quarter

    @pl.when(mine)
    def _():
        for i, total in enumerate(totals):
            mine_ref[i] = total

    @pl.when(jnp.logical_not(mine))
    def _():
        for i, total in enumerate(totals):
            other_ref[i] = total


def split_load(dims, mine_ref, other_ref):
    mine = pl.program_id(0) * dims.per_step < dims.quarter
    return [jnp.where(mine, mine_ref[i], other_ref[i]) for i in range(dims.per_step)]


def leaving_decay(chunks, head, j, run, rows, table_ref, leave_bias_ref):
    return jnp.exp(table_ref[head, pl.ds(chunks + j, 1), :] - run + leave_bias_ref[rows, :])


def begin_kernel(dims, core_ref, own, *rest):
    updates_refs = rest[:-6]
    run_ref, table_ref, gain_ref, weight_bias_ref, enter_bias_ref, leave_bias_ref = rest[-6:]
    chunks = dims.chunks
    p = pl.program_id(0)

    @pl.when(p == 0)
    def _():
        fill_tables(
            chunks, *own.plain, run_ref, table_ref, gain_ref, weight_bias_ref, enter_bias_ref, leave_bias_ref
        )

    k_ref, v_ref = own()[2:]
    first = dims.head(0, p, core_ref) * dims.per_step
    items = items_of(chunks, dims.per_step)
    runs = [columns(run_ref[first + i, :, rows]) for i, j, rows, cols in items]
    leaves = [
        leaving_decay(chunks, first + i, j, run, rows, table_ref, leave_bias_ref)
        for run, (i, j, rows, cols) in zip(runs, items)
    ]
    kds = [(k_ref[rows, cols].astype(F32) * leave).astype(BF16) for leave, (i, j, rows, cols) in zip(leaves, items)]
    updates = [t_dot(kd, v_ref[rows, cols]) for kd, (i, j, rows, cols) in zip(kds, items)]
    totals = []
    for i in range(dims.per_step):
        total = updates[i * chunks]
        for j in range(1, chunks):
            total = table_ref[first + i, pl.ds(j, 1), :] * total + updates[i * chunks + j]
        totals.append(total)
    for at, ref in enumerate(updates_refs):

        @pl.when(p // (dims.steps // 2) == at)
        def _():
            for i, total in enumerate(totals):
                ref[i] = total


def inside_kernel(dims, core_ref, own, *rest):
    q_ref, k_ref, v_ref, run_ref, table_ref, weight_bias_ref, enter_bias_ref, leave_bias_ref = own()
    prefix_ref, inside_ref, qd_ref, kd_ref, vd_ref, attend_ref = rest[-6:]
    chunks = dims.chunks
    items = items_of(chunks, dims.per_step)
    q, k, v = ([ref[rows, cols] for i, j, rows, cols in items] for ref in (q_ref, k_ref, v_ref))
    scores = [dot_t(a, b) for a, b in zip(q, k)]
    marks = [run_ref[i, :, rows] for i, j, rows, cols in items]
    runs = [columns(mark) for mark in marks]
    leaves = [
        leaving_decay(chunks, i, j, run, rows, table_ref, leave_bias_ref)
        for run, (i, j, rows, cols) in zip(runs, items)
    ]
    kds = [(a.astype(F32) * leave).astype(BF16) for a, leave in zip(k, leaves)]
    attends = [
        (score * jnp.exp(run - mark + weight_bias_ref[rows, :])).astype(BF16)
        for score, run, mark, (i, j, rows, cols) in zip(scores, runs, marks, items)
    ]
    updates = [t_dot(kd, b) for kd, b in zip(kds, v)]
    for x, (i, j, rows, cols) in enumerate(items):
        inside_ref[i, rows, :] = dot(attends[x], v[x])
        attend_ref[i, rows, :] = attends[x].T
        kd_ref[i, rows, :] = kds[x]
        vd_ref[i, rows, :] = (v[x].astype(F32) * leaves[x]).astype(BF16)
        qd_ref[i, rows, :] = (q[x].astype(F32) * jnp.exp(runs[x] + enter_bias_ref[rows, :])).astype(BF16)
    for i in range(dims.per_step):
        total = None
        for j in range(chunks - 1):
            update = updates[i * chunks + j]
            total = update if total is None else table_ref[i, j : j + 1, :] * total + update
            prefix_ref[i, j] = total


def entering_states(chunks, i, incoming, table_ref, prefix_ref):
    states, gain = [], None
    for j in range(chunks):
        states.append((incoming if j == 0 else gain * incoming + prefix_ref[i, j - 1]).astype(BF16))
        passing = table_ref[i, j : j + 1, :]
        gain = passing if gain is None else gain * passing
    return states


def leaving_states(chunks, i, outgoing, table_ref, suffix_ref):
    states, gain = [None] * chunks, None
    for j in range(chunks - 1, -1, -1):
        states[j] = (outgoing if j == chunks - 1 else gain * outgoing + suffix_ref[i, j]).astype(BF16)
        passing = table_ref[i, j : j + 1, :]
        gain = passing if gain is None else gain * passing
    return states


def forward_kernel(dims, core_ref, own, *rest):
    inside_ref, qd_ref, og_ref, table_ref, prefix_ref, keep_ref, back_ref = own()
    normed_ref, grad_ref, suffix_ref, mine_ref, other_ref = rest[-5:]
    chunks = dims.chunks
    items = items_of(chunks, dims.per_step)
    states = []
    for i, incoming in enumerate(split_load(dims, keep_ref, back_ref)):
        states += entering_states(chunks, i, incoming, table_ref, prefix_ref)
    outs = [
        inside_ref[i, rows, :] + dot(qd_ref[i, rows, :], state) for state, (i, j, rows, cols) in zip(states, items)
    ]
    squares = [jnp.mean(out * out, axis=-1, keepdims=True) for out in outs]
    ogs = [og_ref[rows, cols].astype(F32) for i, j, rows, cols in items]
    alongs = [jnp.mean(og * out, axis=-1, keepdims=True) for og, out in zip(ogs, outs)]
    factors = [lax.rsqrt(square + EPS) for square in squares]
    grads = []
    for out, factor, og, along, (i, j, rows, cols) in zip(outs, factors, ogs, alongs, items):
        normed = out * factor
        normed_ref[rows, cols] = normed.astype(BF16)
        grad = (factor * (og - (factor * along) * normed)).astype(BF16)
        grad_ref[i, rows, :] = grad
        grads.append(grad)
    parts = [t_dot(qd_ref[i, rows, :], grad) for grad, (i, j, rows, cols) in zip(grads, items)]
    totals = []
    for i in range(dims.per_step):
        total = parts[i * chunks + chunks - 1]
        for j in range(chunks - 2, -1, -1):
            suffix_ref[i, j] = total
            total = table_ref[i, j : j + 1, :] * total + parts[i * chunks + j]
        totals.append(total)
    split_store(dims, mine_ref, other_ref, totals)


def query_kernel(dims, core_ref, own, *rest):
    (
        k_ref, v_ref, grad_ref, run_ref, table_ref, weight_bias_ref, enter_bias_ref, prefix_ref, keep_ref, back_ref
    ) = own()
    dq_ref, dattend_ref = rest[-2:]
    chunks = dims.chunks
    items = items_of(chunks, dims.per_step)
    states = []
    for i, incoming in enumerate(split_load(dims, keep_ref, back_ref)):
        states += entering_states(chunks, i, incoming, table_ref, prefix_ref)
    grads = [grad_ref[i, rows, :] for i, j, rows, cols in items]
    scores = [dot_t(grad, v_ref[rows, cols]) for grad, (i, j, rows, cols) in zip(grads, items)]
    marks = [run_ref[i, :, rows] for i, j, rows, cols in items]
    runs = [columns(mark) for mark in marks]
    dattends = [
        (score * jnp.exp(run - mark + weight_bias_ref[rows, :])).astype(BF16)
        for score, run, mark, (i, j, rows, cols) in zip(scores, runs, marks, items)
    ]
    enters = [jnp.exp(run + enter_bias_ref[rows, :]) for run, (i, j, rows, cols) in zip(runs, items)]
    for x, (i, j, rows, cols) in enumerate(items):
        dattend_ref[i, rows, :] = dattends[x].T
        dq = dot(dattends[x], k_ref[rows, cols]) + enters[x] * dot_t(grads[x], states[x])
        dq_ref[rows, cols] = dq.astype(BF16)


def backward_kernel(dims, core_ref, own, *rest):
    (
        q_ref, grad_ref, attend_ref, dattend_ref, kd_ref, vd_ref, table_ref, suffix_ref, gkeep_ref, gback_ref
    ) = own()
    dk_ref, dv_ref = rest[-2:]
    chunks = dims.chunks
    items = items_of(chunks, dims.per_step)
    states = []
    for i, outgoing in enumerate(split_load(dims, gkeep_ref, gback_ref)):
        states += leaving_states(chunks, i, outgoing, table_ref, suffix_ref)
    for state, (i, j, rows, cols) in zip(states, items):
        dk = dot(dattend_ref[i, rows, :], q_ref[rows, cols]) + dot_t(vd_ref[i, rows, :], state)
        dk_ref[rows, cols] = dk.astype(BF16)
        dv = dot(attend_ref[i, rows, :], grad_ref[i, rows, :]) + dot(kd_ref[i, rows, :], state)
        dv_ref[rows, cols] = dv.astype(BF16)


def after(value, token):
    return value if token is None else lax.optimization_barrier((value, token))[0]


class Dims:
    def __init__(self, size, per_step, chunks, length, dh, heads):
        self.size, self.per_step, self.chunks = size, per_step, chunks
        self.length, self.dh, self.heads = length, dh, heads
        self.quarter = size // 2
        self.steps = size // per_step

    def head(self, group, p, core_ref):
        return (group + p // self.steps) * self.steps + lax.rem(p + core_ref[0] * (self.steps // 2), self.steps)

    def specs(self, group):
        n, halves = self.per_step, self.steps // 2
        length, dh, chunks = self.length, self.dh, self.chunks
        whole = lambda *shape: pl.BlockSpec(shape, lambda p, c: (0,) * len(shape))
        return dict(
            rows=pl.BlockSpec((length, n * dh), lambda p, c: (0, self.head(group, p, c))),
            run=pl.BlockSpec((n, 1, length), lambda p, c: (self.head(group, p, c), 0, 0)),
            table=pl.BlockSpec((n, 2 * chunks, C), lambda p, c: (self.head(group, p, c), 0, 0)),
            bias=whole(length, C),
            states=pl.BlockSpec((n, chunks - 1, dh, dh), lambda p, c: (p, 0, 0, 0)),
            headed=pl.BlockSpec((n, length, dh), lambda p, c: (p, 0, 0)),
            update=[
                pl.BlockSpec((n, dh, dh), lambda p, c, at=at: (jnp.clip(p - at * halves, 0, halves - 1), 0, 0))
                for at in range(2 * self.heads // self.size)
            ],
            mine=pl.BlockSpec((n, dh, dh), lambda p, c: (jnp.minimum(p, halves - 1), 0, 0)),
            other=pl.BlockSpec((n, dh, dh), lambda p, c: (jnp.maximum(p - halves, 0), 0, 0)),
            decay=whole(self.heads, length),
            start=whole(1, length),
            all_run=whole(self.heads, 1, length),
            all_table=whole(self.heads, 2 * chunks, C),
            all_gain=whole(self.heads, C),
            any=pl.BlockSpec(memory_space=pl.ANY),
        )


def with_rows(kernel, dims, group, which, inputs, core_ref, *refs):
    count = len(which)
    slots, sems = refs[len(refs) - 2 * count : len(refs) - count], refs[len(refs) - count :]
    refs = list(refs[: len(refs) - 2 * count])
    p = pl.program_id(0)
    width = dims.per_step * dims.dh

    def copy(x, step):
        start = pl.multiple_of(dims.head(group, step, core_ref) * width, width)
        return pltpu.make_async_copy(refs[which[x]].at[:, pl.ds(start, width)], slots[x].at[step], sems[x].at[step])

    @pl.when(p == 0)
    def _():
        for step in range(slots[0].shape[0]):
            for x in range(count):
                copy(x, step).start()

    def own():
        for x in range(count):
            copy(x, p).wait()
        return [slots[which.index(y)].at[p] if y in which else refs[y] for y in range(inputs)]

    own.plain = [refs[y] for y in range(inputs) if y not in which]
    kernel(dims, core_ref, own, *refs[inputs:])


def call_heads(
    dims, core_arg, kernel, group, in_names, out_names, out_shapes, args, name, products, reads, aliases=(), tokens=(),
    steps=None, stay=(),
):
    specs = dims.specs(group)
    steps = steps or dims.steps
    extra = [a for a in aliases if a is not None]
    which = [x for x, n in enumerate(in_names) if n == "rows"]
    args = [pltpu.with_memory_space_constraint(a, pltpu.HBM) if n in stay else a for n, a in zip(in_names, args)]
    in_specs = [pl.BlockSpec(memory_space=pltpu.HBM) if n == "rows" else specs[n] for n in in_names]
    return pl.pallas_call(
        functools.partial(with_rows, kernel, dims, group, which, len(in_names)),
        grid_spec=pltpu.PrefetchScalarGridSpec(
            num_scalar_prefetch=1,
            grid=(steps,),
            in_specs=in_specs + [specs["any"]] * (len(extra) + len(tokens)),
            out_specs=[s for n in out_names for s in (specs[n] if n == "update" else [specs[n]])],
            scratch_shapes=[pltpu.VMEM((steps, dims.length, dims.per_step * dims.dh), BF16) for _ in which]
            + [pltpu.SemaphoreType.DMA((steps,)) for _ in which],
        ),
        out_shape=out_shapes,
        input_output_aliases={1 + len(in_names) + i: i for i in range(len(extra))},
        compiler_params=pltpu.CompilerParams(
            dimension_semantics=("arbitrary",), vmem_limit_bytes=VMEM_LIMIT
        ),
        cost_estimate=pl.CostEstimate(
            flops=products * dims.size * 2 * dims.length * C * dims.dh,
            bytes_accessed=reads * dims.size * dims.length * dims.dh * 2,
            transcendentals=dims.size * dims.length * C,
        ),
        name=name,
    )(core_arg, *args, *extra, *tokens)


def local(query_in, key_in, value_in, log_decay, doc_start, out_grad):
    length, width = query_in.shape
    heads = log_decay.shape[0]
    dh = width // heads
    chunks = length // C
    groups = GROUPS
    size = heads // groups
    quarter = size // 2
    dims = Dims(size, PER_STEP, chunks, length, dh, heads)
    shards = lax.axis_size("seq")
    core = lax.axis_index("ctx")
    first = core == 0
    core_arg = core.astype(jnp.int32).reshape(1)
    swap = [(0, 1), (1, 0)]
    shape = jax.ShapeDtypeStruct
    states_shape = shape((size, chunks - 1, dh, dh), F32)
    part_shape = shape((quarter, dh, dh), F32)
    rows_shape = shape((length, width), BF16)
    bias_shape = shape((length, C), F32)
    call = functools.partial(call_heads, dims, core_arg)

    headed = lambda kind: shape((size, length, dh), kind)
    *updates, run, table, gain, weight_bias, enter_bias, leave_bias = call(
        begin_kernel, 0,
        ["decay", "start", "rows", "rows"],
        ["update", "all_run", "all_table", "all_gain", "bias", "bias", "bias"],
        (
            *[part_shape] * (2 * groups),
            shape((heads, 1, length), F32), shape((heads, 2 * chunks, C), F32), shape((heads, C), F32),
            bias_shape, bias_shape, bias_shape,
        ),
        (log_decay, doc_start.reshape(1, length), key_in, value_in),
        "begin", 1, 4,
        steps=groups * dims.steps,
        stay=("rows", "decay", "start"),
    )
    gain_other = lax.ppermute(gain, "ctx", swap)
    gain0 = jnp.where(first, gain, gain_other)
    gain1 = jnp.where(first, gain_other, gain)

    def pick(array, group):
        start = group * size + core * quarter
        return lax.dynamic_slice_in_dim(array, start, quarter, 0)[:, None, :]

    class Carry:
        def __init__(self, group, mine, other, backward):
            self.backward = backward
            self.g0, self.g1 = pick(gain0, group), pick(gain1, group)
            self.both = self.g0 * self.g1
            self.mine, self.got = mine, lax.ppermute(other, "ctx", swap)
            if backward:
                self.hops = [(k, k - 1) for k in range(shards - 1, 0, -1)]
            else:
                self.hops = [(k, k + 1) for k in range(shards - 1)]
            self.landed = []

        def start(self, token=None):
            got = after(self.got, token)
            self.zero = jnp.where(first, self.mine, got)
            self.one = jnp.where(first, got, self.mine)
            if self.backward:
                self.total = self.g0 * self.one + self.zero
            else:
                self.total = self.g1 * self.zero + self.one

        def hop(self, index, token=None):
            if index == 0:
                self.start(token)
                self.sent = self.total
            else:
                self.settle(token)
                self.sent = self.both * self.state + self.total
            self.landed.append(lax.ppermute(self.sent, "seq", [self.hops[index]]))

        def settle(self, token=None):
            self.landed[-1] = after(self.landed[-1], token)
            self.state = sum(self.landed[1:], self.landed[0])

        def finish(self, token=None):
            self.settle(token)
            state = self.state
            if self.backward:
                inner = self.g1 * state + self.one
                keep, send = jnp.where(first, inner, state), jnp.where(first, state, inner)
            else:
                inner = self.g0 * state + self.zero
                keep, send = jnp.where(first, state, inner), jnp.where(first, inner, state)
            return keep, lax.ppermute(send, "ctx", swap)

    def inside_of(group, token):
        return call(
            inside_kernel, group,
            ["rows"] * 3 + ["run", "table", "bias", "bias", "bias"],
            ["states"] + ["headed"] * 5,
            (states_shape, headed(F32), headed(BF16), headed(BF16), headed(BF16), headed(BF16)),
            (query_in, key_in, value_in, run, table, weight_bias, enter_bias, leave_bias),
            "inside", 4, 10,
            stay=("rows",),
            tokens=[token],
        )

    hops = range(shards - 1)
    carries = [Carry(group, updates[2 * group], updates[2 * group + 1], False) for group in range(groups)]
    insides = []
    token = None
    for index in hops:
        for carry in carries:
            carry.hop(index, token)
            token = carry.sent
        while index == min(1, shards - 2) and len(insides) < groups:
            insides.append(inside_of(len(insides), token))
            token = insides[-1][0]

    normed = None
    incoming, middles, backs = [], [], []
    for group in range(groups):
        incoming.append(carries[group].finish(token))
        prefix, inside, qd = insides[group][:3]
        normed, grad, suffix, mine, other = call(
            forward_kernel, group,
            ["headed", "headed", "rows", "table", "states", "mine", "other"],
            ["rows", "headed", "states", "mine", "other"],
            (rows_shape, headed(BF16), states_shape, part_shape, part_shape),
            (inside, qd, out_grad, table, prefix, *incoming[group]),
            "forward", 2, 8,
            aliases=(normed,),
            tokens=[backs[-1].sent] if backs else [],
        )
        token = mine
        middles.append((grad, suffix))
        backs.append(Carry(group, mine, other, True))
        if group == 0:
            backs[0].hop(0)

    query_gradient = None
    dattends = []

    def query_of(group, token):
        return call(
            query_kernel, group,
            ["rows", "rows", "headed", "run", "table", "bias", "bias", "states", "mine", "other"],
            ["rows", "headed"],
            (rows_shape, headed(BF16)),
            (
                key_in, value_in, middles[group][0], run, table, weight_bias, enter_bias, insides[group][0],
                *incoming[group],
            ),
            "query", 3, 8,
            aliases=(query_gradient,),
            tokens=[token],
        )

    for index in hops:
        for place, back in enumerate(backs):
            ahead = index + 1 if place == 0 else index
            if ahead in hops:
                back.hop(ahead, token)
                token = back.sent
        while index == min(1, shards - 2) and len(dattends) < groups:
            query_gradient, dattend = query_of(len(dattends), token)
            dattends.append(dattend)
            token = dattend
    grads = (None, None)
    for group in range(groups):
        grad, suffix = middles[group]
        kd, vd, attend = insides[group][3:]
        grads = call(
            backward_kernel, group,
            ["rows"] + ["headed"] * 5 + ["table", "states", "mine", "other"],
            ["rows", "rows"],
            (rows_shape, rows_shape),
            (query_in, grad, attend, dattends[group], kd, vd, table, suffix, *backs[group].finish(token)),
            "backward", 4, 10,
            aliases=grads,
        )
        token = grads[0]
    return (normed, query_gradient, *grads)


def solution(mesh):
    rows = P(("groups", "seq", "ctx"), "tensor")
    return jax.shard_map(
        local,
        mesh=mesh,
        in_specs=(rows, rows, rows, P("tensor", ("groups", "seq", "ctx")), P(("groups", "seq", "ctx")), rows),
        out_specs=(rows, rows, rows, rows),
        check_vma=False,
    )
```

```python
import functools

import jax
import jax.numpy as jnp
from jax import lax
from jax.experimental import pallas as pl
from jax.experimental.pallas import tpu as pltpu
from jax.sharding import PartitionSpec as P

C = 128
EPS = 1e-06
NEG = -1e30
GROUPS = 2
PER_STEP = 2
F32 = jnp.float32
BF16 = jnp.bfloat16
VMEM_LIMIT = 20 * 1024 * 1024


def dot(a, b):
    return lax.dot_general(a, b, (((1,), (0,)), ((), ())), preferred_element_type=F32)


def dot_t(a, b):
    return lax.dot_general(a, b, (((1,), (1,)), ((), ())), preferred_element_type=F32)


def t_dot(a, b):
    return lax.dot_general(a, b, (((0,), (0,)), ((), ())), preferred_element_type=F32)


def exact_dot(a, b):
    return lax.dot_general(
        a, b, (((1,), (0,)), ((), ())), precision=lax.Precision.HIGHEST, preferred_element_type=F32
    )


def columns(row):
    return jnp.broadcast_to(row, (C, C)).T


def fill_tables(chunks, decay_ref, start_ref, run_ref, table_ref, gain_ref, weight_bias_ref, enter_bias_ref, leave_bias_ref):
    heads = decay_ref.shape[0]
    at_row = lax.broadcasted_iota(jnp.int32, (C, C), 0)
    at_lane = lax.broadcasted_iota(jnp.int32, (C, C), 1)
    upper = jnp.where(at_row <= at_lane, 1.0, 0.0).astype(F32)
    sums = jnp.concatenate([upper, jnp.ones((C, C), F32)], axis=1)
    gain = jnp.ones((heads, C), F32)
    each = range(chunks)
    spans = [pl.ds(j * C, C) for j in each]
    runs = [exact_dot(decay_ref[:, span], sums) for span in spans]
    starts = jnp.concatenate([start_ref[:, span].astype(F32) for span in spans] * (8 // chunks), axis=0)
    docs_all = dot(starts.astype(BF16), sums.astype(BF16))
    for j in each:
        span = spans[j]
        last = runs[j][:, C:]
        docs, docs_last = docs_all[j : j + 1, :C], docs_all[j : j + 1, C:]
        passing = jnp.where(docs_last == 0.0, jnp.exp(last), 0.0)
        gain = gain * passing
        run_ref[:, 0, span] = runs[j][:, :C]
        table_ref[:, j, :] = passing
        table_ref[:, chunks + j, :] = last
        docs_column = columns(docs)
        weight_bias_ref[span, :] = jnp.where((docs_column == docs) & (at_lane <= at_row), 0.0, NEG)
        enter_bias_ref[span, :] = jnp.where(docs_column == 0.0, 0.0, NEG)
        leave_bias_ref[span, :] = jnp.where(docs_column == docs_last, 0.0, NEG)
    gain_ref[...] = gain


def items_of(chunks, per_step):
    return [(i, j, pl.ds(j * C, C), pl.ds(i * C, C)) for i in range(per_step) for j in range(chunks)]


def split_store(dims, mine_ref, other_ref, totals):
    mine = pl.program_id(0) * dims.per_step < dims.quarter

    @pl.when(mine)
    def _():
        for i, total in enumerate(totals):
            mine_ref[i] = total

    @pl.when(jnp.logical_not(mine))
    def _():
        for i, total in enumerate(totals):
            other_ref[i] = total


def split_load(dims, mine_ref, other_ref):
    mine = pl.program_id(0) * dims.per_step < dims.quarter
    return [jnp.where(mine, mine_ref[i], other_ref[i]) for i in range(dims.per_step)]


def leaving_decay(chunks, head, j, run, rows, table_ref, leave_bias_ref):
    return jnp.exp(table_ref[head, pl.ds(chunks + j, 1), :] - run + leave_bias_ref[rows, :])


def begin_kernel(dims, core_ref, own, *rest):
    updates_refs, place_ref = rest[:-7], rest[-7]
    run_ref, table_ref, gain_ref, weight_bias_ref, enter_bias_ref, leave_bias_ref = rest[-6:]
    chunks = dims.chunks
    p = pl.program_id(0)

    @pl.when(p == 0)
    def _():
        place_ref[...] = jnp.where(lax.broadcasted_iota(jnp.int32, place_ref.shape, 0) == core_ref[1], 1.0, 0.0)
        fill_tables(
            chunks, *own.plain, run_ref, table_ref, gain_ref, weight_bias_ref, enter_bias_ref, leave_bias_ref
        )

    k_ref, v_ref = own()[2:]
    first = dims.head(0, p, core_ref) * dims.per_step
    items = items_of(chunks, dims.per_step)
    runs = [columns(run_ref[first + i, :, rows]) for i, j, rows, cols in items]
    leaves = [
        leaving_decay(chunks, first + i, j, run, rows, table_ref, leave_bias_ref)
        for run, (i, j, rows, cols) in zip(runs, items)
    ]
    kds = [(k_ref[rows, cols].astype(F32) * leave).astype(BF16) for leave, (i, j, rows, cols) in zip(leaves, items)]
    updates = [t_dot(kd, v_ref[rows, cols]) for kd, (i, j, rows, cols) in zip(kds, items)]
    totals = []
    for i in range(dims.per_step):
        total = updates[i * chunks]
        for j in range(1, chunks):
            total = table_ref[first + i, pl.ds(j, 1), :] * total + updates[i * chunks + j]
        totals.append(total)
    for at, ref in enumerate(updates_refs):

        @pl.when(p // (dims.steps // 2) == at)
        def _():
            for i, total in enumerate(totals):
                ref[i] = total


def inside_kernel(dims, core_ref, own, *rest):
    q_ref, k_ref, v_ref, run_ref, table_ref, weight_bias_ref, enter_bias_ref, leave_bias_ref = own()
    prefix_ref, inside_ref, qd_ref, kd_ref, vd_ref, attend_ref = rest[-6:]
    chunks = dims.chunks
    items = items_of(chunks, dims.per_step)
    q, k, v = ([ref[rows, cols] for i, j, rows, cols in items] for ref in (q_ref, k_ref, v_ref))
    scores = [dot_t(a, b) for a, b in zip(q, k)]
    marks = [run_ref[i, :, rows] for i, j, rows, cols in items]
    runs = [columns(mark) for mark in marks]
    leaves = [
        leaving_decay(chunks, i, j, run, rows, table_ref, leave_bias_ref)
        for run, (i, j, rows, cols) in zip(runs, items)
    ]
    kds = [(a.astype(F32) * leave).astype(BF16) for a, leave in zip(k, leaves)]
    attends = [
        (score * jnp.exp(run - mark + weight_bias_ref[rows, :])).astype(BF16)
        for score, run, mark, (i, j, rows, cols) in zip(scores, runs, marks, items)
    ]
    updates = [t_dot(kd, b) for kd, b in zip(kds, v)]
    for x, (i, j, rows, cols) in enumerate(items):
        inside_ref[i, rows, :] = dot(attends[x], v[x])
        attend_ref[i, rows, :] = attends[x].T
        kd_ref[i, rows, :] = kds[x]
        vd_ref[i, rows, :] = (v[x].astype(F32) * leaves[x]).astype(BF16)
        qd_ref[i, rows, :] = (q[x].astype(F32) * jnp.exp(runs[x] + enter_bias_ref[rows, :])).astype(BF16)
    for i in range(dims.per_step):
        total = None
        for j in range(chunks - 1):
            update = updates[i * chunks + j]
            total = update if total is None else table_ref[i, j : j + 1, :] * total + update
            prefix_ref[i, j] = total


def entering_states(chunks, i, incoming, table_ref, prefix_ref):
    states, gain = [], None
    for j in range(chunks):
        states.append((incoming if j == 0 else gain * incoming + prefix_ref[i, j - 1]).astype(BF16))
        passing = table_ref[i, j : j + 1, :]
        gain = passing if gain is None else gain * passing
    return states


def leaving_states(chunks, i, outgoing, table_ref, suffix_ref):
    states, gain = [None] * chunks, None
    for j in range(chunks - 1, -1, -1):
        states[j] = (outgoing if j == chunks - 1 else gain * outgoing + suffix_ref[i, j]).astype(BF16)
        passing = table_ref[i, j : j + 1, :]
        gain = passing if gain is None else gain * passing
    return states


def forward_kernel(dims, core_ref, own, *rest):
    inside_ref, qd_ref, og_ref, table_ref, prefix_ref, keep_ref, back_ref = own()
    normed_ref, grad_ref, suffix_ref, mine_ref, other_ref = rest[-5:]
    chunks = dims.chunks
    items = items_of(chunks, dims.per_step)
    states = []
    for i, incoming in enumerate(split_load(dims, keep_ref, back_ref)):
        states += entering_states(chunks, i, incoming, table_ref, prefix_ref)
    outs = [
        inside_ref[i, rows, :] + dot(qd_ref[i, rows, :], state) for state, (i, j, rows, cols) in zip(states, items)
    ]
    squares = [jnp.mean(out * out, axis=-1, keepdims=True) for out in outs]
    ogs = [og_ref[rows, cols].astype(F32) for i, j, rows, cols in items]
    alongs = [jnp.mean(og * out, axis=-1, keepdims=True) for og, out in zip(ogs, outs)]
    factors = [lax.rsqrt(square + EPS) for square in squares]
    grads = []
    for out, factor, og, along, (i, j, rows, cols) in zip(outs, factors, ogs, alongs, items):
        normed = out * factor
        normed_ref[rows, cols] = normed.astype(BF16)
        grad = (factor * (og - (factor * along) * normed)).astype(BF16)
        grad_ref[i, rows, :] = grad
        grads.append(grad)
    parts = [t_dot(qd_ref[i, rows, :], grad) for grad, (i, j, rows, cols) in zip(grads, items)]
    totals = []
    for i in range(dims.per_step):
        total = parts[i * chunks + chunks - 1]
        for j in range(chunks - 2, -1, -1):
            suffix_ref[i, j] = total
            total = table_ref[i, j : j + 1, :] * total + parts[i * chunks + j]
        totals.append(total)
    split_store(dims, mine_ref, other_ref, totals)


def query_kernel(dims, core_ref, own, *rest):
    (
        k_ref, v_ref, grad_ref, run_ref, table_ref, weight_bias_ref, enter_bias_ref, prefix_ref, keep_ref, back_ref
    ) = own()
    dq_ref, dattend_ref = rest[-2:]
    chunks = dims.chunks
    items = items_of(chunks, dims.per_step)
    states = []
    for i, incoming in enumerate(split_load(dims, keep_ref, back_ref)):
        states += entering_states(chunks, i, incoming, table_ref, prefix_ref)
    grads = [grad_ref[i, rows, :] for i, j, rows, cols in items]
    scores = [dot_t(grad, v_ref[rows, cols]) for grad, (i, j, rows, cols) in zip(grads, items)]
    marks = [run_ref[i, :, rows] for i, j, rows, cols in items]
    runs = [columns(mark) for mark in marks]
    dattends = [
        (score * jnp.exp(run - mark + weight_bias_ref[rows, :])).astype(BF16)
        for score, run, mark, (i, j, rows, cols) in zip(scores, runs, marks, items)
    ]
    enters = [jnp.exp(run + enter_bias_ref[rows, :]) for run, (i, j, rows, cols) in zip(runs, items)]
    for x, (i, j, rows, cols) in enumerate(items):
        dattend_ref[i, rows, :] = dattends[x].T
        dq = dot(dattends[x], k_ref[rows, cols]) + enters[x] * dot_t(grads[x], states[x])
        dq_ref[rows, cols] = dq.astype(BF16)


def backward_kernel(dims, core_ref, own, *rest):
    (
        q_ref, grad_ref, attend_ref, dattend_ref, kd_ref, vd_ref, table_ref, suffix_ref, gkeep_ref, gback_ref
    ) = own()
    dk_ref, dv_ref = rest[-2:]
    chunks = dims.chunks
    items = items_of(chunks, dims.per_step)
    states = []
    for i, outgoing in enumerate(split_load(dims, gkeep_ref, gback_ref)):
        states += leaving_states(chunks, i, outgoing, table_ref, suffix_ref)
    for state, (i, j, rows, cols) in zip(states, items):
        dk = dot(dattend_ref[i, rows, :], q_ref[rows, cols]) + dot_t(vd_ref[i, rows, :], state)
        dk_ref[rows, cols] = dk.astype(BF16)
        dv = dot(attend_ref[i, rows, :], grad_ref[i, rows, :]) + dot(kd_ref[i, rows, :], state)
        dv_ref[rows, cols] = dv.astype(BF16)


def after(value, token):
    return value if token is None else lax.optimization_barrier((value, token))[0]


class Dims:
    def __init__(self, size, per_step, chunks, length, dh, heads, shards):
        self.size, self.per_step, self.chunks = size, per_step, chunks
        self.length, self.dh, self.heads = length, dh, heads
        self.quarter = size // 2
        self.steps = size // per_step
        self.places = -(-shards // 8) * 8

    def head(self, group, p, core_ref):
        return (group + p // self.steps) * self.steps + lax.rem(p + core_ref[0] * (self.steps // 2), self.steps)

    def specs(self, group):
        n, halves = self.per_step, self.steps // 2
        length, dh, chunks = self.length, self.dh, self.chunks
        whole = lambda *shape: pl.BlockSpec(shape, lambda p, c: (0,) * len(shape))
        return dict(
            rows=pl.BlockSpec((length, n * dh), lambda p, c: (0, self.head(group, p, c))),
            run=pl.BlockSpec((n, 1, length), lambda p, c: (self.head(group, p, c), 0, 0)),
            table=pl.BlockSpec((n, 2 * chunks, C), lambda p, c: (self.head(group, p, c), 0, 0)),
            bias=whole(length, C),
            states=pl.BlockSpec((n, chunks - 1, dh, dh), lambda p, c: (p, 0, 0, 0)),
            headed=pl.BlockSpec((n, length, dh), lambda p, c: (p, 0, 0)),
            update=[
                pl.BlockSpec((n, dh, dh), lambda p, c, at=at: (jnp.clip(p - at * halves, 0, halves - 1), 0, 0))
                for at in range(2 * self.heads // self.size)
            ],
            mine=pl.BlockSpec((n, dh, dh), lambda p, c: (jnp.minimum(p, halves - 1), 0, 0)),
            other=pl.BlockSpec((n, dh, dh), lambda p, c: (jnp.maximum(p - halves, 0), 0, 0)),
            decay=whole(self.heads, length),
            start=whole(1, length),
            all_run=whole(self.heads, 1, length),
            all_table=whole(self.heads, 2 * chunks, C),
            all_gain=whole(self.heads, C),
            place=whole(self.places, C),
            any=pl.BlockSpec(memory_space=pl.ANY),
        )


def with_rows(kernel, dims, group, which, inputs, core_ref, *refs):
    count = len(which)
    slots, sems = refs[len(refs) - 2 * count : len(refs) - count], refs[len(refs) - count :]
    refs = list(refs[: len(refs) - 2 * count])
    p = pl.program_id(0)
    width = dims.per_step * dims.dh

    def copy(x, step):
        start = pl.multiple_of(dims.head(group, step, core_ref) * width, width)
        return pltpu.make_async_copy(refs[which[x]].at[:, pl.ds(start, width)], slots[x].at[step], sems[x].at[step])

    @pl.when(p == 0)
    def _():
        for step in range(slots[0].shape[0]):
            for x in range(count):
                copy(x, step).start()

    def own():
        for x in range(count):
            copy(x, p).wait()
        return [slots[which.index(y)].at[p] if y in which else refs[y] for y in range(inputs)]

    own.plain = [refs[y] for y in range(inputs) if y not in which]
    kernel(dims, core_ref, own, *refs[inputs:])


def call_heads(
    dims, core_arg, kernel, group, in_names, out_names, out_shapes, args, name, products, reads, aliases=(), tokens=(),
    steps=None, stay=(),
):
    specs = dims.specs(group)
    steps = steps or dims.steps
    extra = [a for a in aliases if a is not None]
    which = [x for x, n in enumerate(in_names) if n == "rows"]
    args = [pltpu.with_memory_space_constraint(a, pltpu.HBM) if n in stay else a for n, a in zip(in_names, args)]
    in_specs = [pl.BlockSpec(memory_space=pltpu.HBM) if n == "rows" else specs[n] for n in in_names]
    return pl.pallas_call(
        functools.partial(with_rows, kernel, dims, group, which, len(in_names)),
        grid_spec=pltpu.PrefetchScalarGridSpec(
            num_scalar_prefetch=1,
            grid=(steps,),
            in_specs=in_specs + [specs["any"]] * (len(extra) + len(tokens)),
            out_specs=[s for n in out_names for s in (specs[n] if n == "update" else [specs[n]])],
            scratch_shapes=[pltpu.VMEM((steps, dims.length, dims.per_step * dims.dh), BF16) for _ in which]
            + [pltpu.SemaphoreType.DMA((steps,)) for _ in which],
        ),
        out_shape=out_shapes,
        input_output_aliases={1 + len(in_names) + i: i for i in range(len(extra))},
        compiler_params=pltpu.CompilerParams(
            dimension_semantics=("arbitrary",), vmem_limit_bytes=VMEM_LIMIT
        ),
        cost_estimate=pl.CostEstimate(
            flops=products * dims.size * 2 * dims.length * C * dims.dh,
            bytes_accessed=reads * dims.size * dims.length * dims.dh * 2,
            transcendentals=dims.size * dims.length * C,
        ),
        name=name,
    )(core_arg, *args, *extra, *tokens)


def local(query_in, key_in, value_in, log_decay, doc_start, out_grad):
    length, width = query_in.shape
    heads = log_decay.shape[0]
    dh = width // heads
    chunks = length // C
    groups = GROUPS
    size = heads // groups
    quarter = size // 2
    shards = lax.axis_size("seq")
    dims = Dims(size, PER_STEP, chunks, length, dh, heads, shards)
    core = lax.axis_index("ctx")
    first = core == 0
    core_arg = jnp.stack([core, lax.axis_index("seq")]).astype(jnp.int32)
    swap = [(0, 1), (1, 0)]
    shape = jax.ShapeDtypeStruct
    states_shape = shape((size, chunks - 1, dh, dh), F32)
    part_shape = shape((quarter, dh, dh), F32)
    rows_shape = shape((length, width), BF16)
    bias_shape = shape((length, C), F32)
    call = functools.partial(call_heads, dims, core_arg)

    headed = lambda kind: shape((size, length, dh), kind)
    *updates, places, run, table, gain, weight_bias, enter_bias, leave_bias = call(
        begin_kernel, 0,
        ["decay", "start", "rows", "rows"],
        ["update", "place", "all_run", "all_table", "all_gain", "bias", "bias", "bias"],
        (
            *[part_shape] * (2 * groups),
            shape((dims.places, C), F32),
            shape((heads, 1, length), F32), shape((heads, 2 * chunks, C), F32), shape((heads, C), F32),
            bias_shape, bias_shape, bias_shape,
        ),
        (log_decay, doc_start.reshape(1, length), key_in, value_in),
        "begin", 1, 4,
        steps=groups * dims.steps,
        stay=("rows", "decay", "start"),
    )
    gain_other = lax.ppermute(gain, "ctx", swap)
    gain0 = jnp.where(first, gain, gain_other)
    gain1 = jnp.where(first, gain_other, gain)

    def pick(array, group):
        start = group * size + core * quarter
        return lax.dynamic_slice_in_dim(array, start, quarter, 0)[:, None, :]

    class Carry:
        def __init__(self, group, mine, other, backward):
            self.backward = backward
            self.g0, self.g1 = pick(gain0, group), pick(gain1, group)
            self.both = self.g0 * self.g1
            self.mine, self.got = mine, lax.ppermute(other, "ctx", swap)

        def start(self, token=None):
            got = after(self.got, token)
            self.zero = jnp.where(first, self.mine, got)
            self.one = jnp.where(first, got, self.mine)
            if self.backward:
                self.total = self.g0 * self.one + self.zero
            else:
                self.total = self.g1 * self.zero + self.one

        def finish(self, state):
            if self.backward:
                inner = self.g1 * state + self.one
                keep, send = jnp.where(first, inner, state), jnp.where(first, state, inner)
            else:
                inner = self.g0 * state + self.zero
                keep, send = jnp.where(first, state, inner), jnp.where(first, inner, state)
            return keep, lax.ppermute(send, "ctx", swap)

    class Line:
        def __init__(self, backward):
            self.at = (lambda i: shards - 1 - i) if backward else (lambda i: i)
            self.landed = []

        def step(self, carries, token=None):
            s = len(self.landed)
            sent = None
            for group, carry in enumerate(carries):
                if s - shards + 1 < group <= s:
                    if group == s:
                        carry.start(token)
                        new = carry.total
                    else:
                        new = carry.both * self.last(token) + carry.total
                        token = new
                    sent = new if sent is None else jnp.where(self.here(s - group), new, sent)
            pairs = [(self.at(i), self.at(i + 1)) for i in range(shards - 1) if 0 <= s - i < groups]
            self.landed.append(lax.ppermute(sent, "seq", pairs))
            return sent

        def last(self, token=None):
            self.landed[-1] = after(self.landed[-1], token)
            return self.landed[-1]

        def state(self, group, token=None):
            self.last(token)
            state = self.landed[group + shards - 2]
            for i in range(1, shards - 1):
                state = jnp.where(self.here(i), self.landed[group + i - 1], state)
            return jnp.where(self.here(0), 0.0, state)

        def here(self, i):
            return places[None, self.at(i) : self.at(i) + 1, :] != 0.0

    def inside_of(group, token):
        return call(
            inside_kernel, group,
            ["rows"] * 3 + ["run", "table", "bias", "bias", "bias"],
            ["states"] + ["headed"] * 5,
            (states_shape, headed(F32), headed(BF16), headed(BF16), headed(BF16), headed(BF16)),
            (query_in, key_in, value_in, run, table, weight_bias, enter_bias, leave_bias),
            "inside", 4, 10,
            stay=("rows",),
            tokens=[token],
        )

    carries = [Carry(group, updates[2 * group], updates[2 * group + 1], False) for group in range(groups)]
    line = Line(False)
    insides = []
    token = None
    for index in range(shards - 1):
        token = line.step(carries, token)
        if len(insides) < groups:
            insides.append(inside_of(len(insides), token))
            token = insides[-1][0]
    while len(insides) < groups:
        insides.append(inside_of(len(insides), token))
        token = insides[-1][0]

    normed = None
    incoming, middles, backs = [], [], []
    back_line = Line(True)
    for group in range(groups):
        state = line.state(group, token)
        if group < groups - 1:
            line.step(carries)
        incoming.append(carries[group].finish(state))
        prefix, inside, qd = insides[group][:3]
        normed, grad, suffix, mine, other = call(
            forward_kernel, group,
            ["headed", "headed", "rows", "table", "states", "mine", "other"],
            ["rows", "headed", "states", "mine", "other"],
            (rows_shape, headed(BF16), states_shape, part_shape, part_shape),
            (inside, qd, out_grad, table, prefix, *incoming[group]),
            "forward", 2, 8,
            aliases=(normed,),
            tokens=[sent] if backs else [],
        )
        token = mine
        middles.append((grad, suffix))
        backs.append(Carry(group, mine, other, True))
        if group < groups - 1:
            sent = back_line.step(backs, token if group else None)

    query_gradient = None
    dattends = []

    def query_of(group, token):
        return call(
            query_kernel, group,
            ["rows", "rows", "headed", "run", "table", "bias", "bias", "states", "mine", "other"],
            ["rows", "headed"],
            (rows_shape, headed(BF16)),
            (
                key_in, value_in, middles[group][0], run, table, weight_bias, enter_bias, insides[group][0],
                *incoming[group],
            ),
            "query", 3, 8,
            aliases=(query_gradient,),
            tokens=[token],
        )

    while len(back_line.landed) < shards - 1 or len(dattends) < groups:
        if len(back_line.landed) < shards - 1:
            token = back_line.step(backs, token)
        if len(dattends) < groups:
            query_gradient, dattend = query_of(len(dattends), token)
            dattends.append(dattend)
            token = dattend

    grads = (None, None)
    for group in range(groups):
        state = back_line.state(group, token)
        if group < groups - 1:
            back_line.step(backs)
        grad, suffix = middles[group]
        kd, vd, attend = insides[group][3:]
        grads = call(
            backward_kernel, group,
            ["rows"] + ["headed"] * 5 + ["table", "states", "mine", "other"],
            ["rows", "rows"],
            (rows_shape, rows_shape),
            (query_in, grad, attend, dattends[group], kd, vd, table, suffix, *backs[group].finish(state)),
            "backward", 4, 10,
            aliases=grads,
        )
        token = grads[0]
    return (normed, query_gradient, *grads)


def solution(mesh):
    rows = P(("groups", "seq", "ctx"), "tensor")
    return jax.shard_map(
        local,
        mesh=mesh,
        in_specs=(rows, rows, rows, P("tensor", ("groups", "seq", "ctx")), P(("groups", "seq", "ctx")), rows),
        out_specs=(rows, rows, rows, rows),
        check_vma=False,
    )
```

```python
import functools

import jax
import jax.numpy as jnp
from jax import lax
from jax.experimental import pallas as pl
from jax.experimental.pallas import tpu as pltpu
from jax.sharding import PartitionSpec as P

C = 128
EPS = 1e-06
NEG = -1e30
GROUPS = 2
PER_STEP = 4
F32 = jnp.float32
BF16 = jnp.bfloat16
VMEM_LIMIT = 20 * 1024 * 1024


def dot(a, b):
    return lax.dot_general(a, b, (((1,), (0,)), ((), ())), preferred_element_type=F32)


def dot_t(a, b):
    return lax.dot_general(a, b, (((1,), (1,)), ((), ())), preferred_element_type=F32)


def t_dot(a, b):
    return lax.dot_general(a, b, (((0,), (0,)), ((), ())), preferred_element_type=F32)


def exact_dot(a, b):
    return lax.dot_general(
        a, b, (((1,), (0,)), ((), ())), precision=lax.Precision.HIGHEST, preferred_element_type=F32
    )


def columns(row):
    return jnp.broadcast_to(row, (C, C)).T


def fill_tables(chunks, decay_ref, start_ref, run_ref, table_ref, gain_ref, weight_bias_ref, enter_bias_ref, leave_bias_ref):
    heads = decay_ref.shape[0]
    at_row = lax.broadcasted_iota(jnp.int32, (C, C), 0)
    at_lane = lax.broadcasted_iota(jnp.int32, (C, C), 1)
    upper = jnp.where(at_row <= at_lane, 1.0, 0.0).astype(F32)
    sums = jnp.concatenate([upper, jnp.ones((C, C), F32)], axis=1)
    gain = jnp.ones((heads, C), F32)
    each = range(chunks)
    spans = [pl.ds(j * C, C) for j in each]
    runs = [exact_dot(decay_ref[:, span], sums) for span in spans]
    starts = jnp.concatenate([start_ref[:, span].astype(F32) for span in spans] * (8 // chunks), axis=0)
    docs_all = dot(starts.astype(BF16), sums.astype(BF16))
    for j in each:
        span = spans[j]
        last = runs[j][:, C:]
        docs, docs_last = docs_all[j : j + 1, :C], docs_all[j : j + 1, C:]
        passing = jnp.where(docs_last == 0.0, jnp.exp(last), 0.0)
        gain = gain * passing
        run_ref[:, 0, span] = runs[j][:, :C]
        table_ref[:, j, :] = passing
        table_ref[:, chunks + j, :] = last
        docs_column = columns(docs)
        weight_bias_ref[span, :] = jnp.where((docs_column == docs) & (at_lane <= at_row), 0.0, NEG)
        enter_bias_ref[span, :] = jnp.where(docs_column == 0.0, 0.0, NEG)
        leave_bias_ref[span, :] = jnp.where(docs_column == docs_last, 0.0, NEG)
    gain_ref[...] = gain


def items_of(chunks, per_step):
    return [(i, j, pl.ds(j * C, C), pl.ds(i * C, C)) for i in range(per_step) for j in range(chunks)]


def split_store(dims, mine_ref, other_ref, totals):
    mine = pl.program_id(0) * dims.per_step < dims.quarter

    @pl.when(mine)
    def _():
        for i, total in enumerate(totals):
            mine_ref[i] = total

    @pl.when(jnp.logical_not(mine))
    def _():
        for i, total in enumerate(totals):
            other_ref[i] = total


def split_load(dims, mine_ref, other_ref):
    mine = pl.program_id(0) * dims.per_step < dims.quarter
    return [jnp.where(mine, mine_ref[i], other_ref[i]) for i in range(dims.per_step)]


def leaving_decay(chunks, head, j, run, rows, table_ref, leave_bias_ref):
    return jnp.exp(table_ref[head, pl.ds(chunks + j, 1), :] - run + leave_bias_ref[rows, :])


def begin_kernel(dims, core_ref, own, *rest):
    updates_refs = rest[:-6]
    run_ref, table_ref, gain_ref, weight_bias_ref, enter_bias_ref, leave_bias_ref = rest[-6:]
    chunks = dims.chunks
    p = pl.program_id(0)

    @pl.when(p == 0)
    def _():
        fill_tables(
            chunks, *own.plain, run_ref, table_ref, gain_ref, weight_bias_ref, enter_bias_ref, leave_bias_ref
        )

    k_ref, v_ref = own()[2:]
    first = dims.head(0, p, core_ref) * dims.per_step
    items = items_of(chunks, dims.per_step)
    runs = [columns(run_ref[first + i, :, rows]) for i, j, rows, cols in items]
    leaves = [
        leaving_decay(chunks, first + i, j, run, rows, table_ref, leave_bias_ref)
        for run, (i, j, rows, cols) in zip(runs, items)
    ]
    kds = [(k_ref[rows, cols].astype(F32) * leave).astype(BF16) for leave, (i, j, rows, cols) in zip(leaves, items)]
    updates = [t_dot(kd, v_ref[rows, cols]) for kd, (i, j, rows, cols) in zip(kds, items)]
    totals = []
    for i in range(dims.per_step):
        total = updates[i * chunks]
        for j in range(1, chunks):
            total = table_ref[first + i, pl.ds(j, 1), :] * total + updates[i * chunks + j]
        totals.append(total)
    for at, ref in enumerate(updates_refs):

        @pl.when(p // (dims.steps // 2) == at)
        def _():
            for i, total in enumerate(totals):
                ref[i] = total


def inside_kernel(dims, core_ref, own, *rest):
    q_ref, k_ref, v_ref, run_ref, table_ref, weight_bias_ref, enter_bias_ref, leave_bias_ref = own()
    prefix_ref, inside_ref, qd_ref, kd_ref, vd_ref, attend_ref = rest[-6:]
    chunks = dims.chunks
    items = items_of(chunks, dims.per_step)
    q, k, v = ([ref[rows, cols] for i, j, rows, cols in items] for ref in (q_ref, k_ref, v_ref))
    scores = [dot_t(a, b) for a, b in zip(q, k)]
    marks = [run_ref[i, :, rows] for i, j, rows, cols in items]
    runs = [columns(mark) for mark in marks]
    leaves = [
        leaving_decay(chunks, i, j, run, rows, table_ref, leave_bias_ref)
        for run, (i, j, rows, cols) in zip(runs, items)
    ]
    kds = [(a.astype(F32) * leave).astype(BF16) for a, leave in zip(k, leaves)]
    attends = [
        (score * jnp.exp(run - mark + weight_bias_ref[rows, :])).astype(BF16)
        for score, run, mark, (i, j, rows, cols) in zip(scores, runs, marks, items)
    ]
    updates = [t_dot(kd, b) for kd, b in zip(kds, v)]
    for x, (i, j, rows, cols) in enumerate(items):
        inside_ref[i, rows, :] = dot(attends[x], v[x])
        attend_ref[i, rows, :] = attends[x].T
        kd_ref[i, rows, :] = kds[x]
        vd_ref[i, rows, :] = (v[x].astype(F32) * leaves[x]).astype(BF16)
        qd_ref[i, rows, :] = (q[x].astype(F32) * jnp.exp(runs[x] + enter_bias_ref[rows, :])).astype(BF16)
    for i in range(dims.per_step):
        total = None
        for j in range(chunks - 1):
            update = updates[i * chunks + j]
            total = update if total is None else table_ref[i, j : j + 1, :] * total + update
            prefix_ref[i, j] = total


def entering_states(chunks, i, incoming, table_ref, prefix_ref):
    states, gain = [], None
    for j in range(chunks):
        states.append((incoming if j == 0 else gain * incoming + prefix_ref[i, j - 1]).astype(BF16))
        passing = table_ref[i, j : j + 1, :]
        gain = passing if gain is None else gain * passing
    return states


def leaving_states(chunks, i, outgoing, table_ref, suffix_ref):
    states, gain = [None] * chunks, None
    for j in range(chunks - 1, -1, -1):
        states[j] = (outgoing if j == chunks - 1 else gain * outgoing + suffix_ref[i, j]).astype(BF16)
        passing = table_ref[i, j : j + 1, :]
        gain = passing if gain is None else gain * passing
    return states


def forward_kernel(dims, core_ref, own, *rest):
    inside_ref, qd_ref, og_ref, table_ref, prefix_ref, keep_ref, back_ref = own()
    normed_ref, grad_ref, suffix_ref, mine_ref, other_ref = rest[-5:]
    chunks = dims.chunks
    items = items_of(chunks, dims.per_step)
    states = []
    for i, incoming in enumerate(split_load(dims, keep_ref, back_ref)):
        states += entering_states(chunks, i, incoming, table_ref, prefix_ref)
    outs = [
        inside_ref[i, rows, :] + dot(qd_ref[i, rows, :], state) for state, (i, j, rows, cols) in zip(states, items)
    ]
    squares = [jnp.mean(out * out, axis=-1, keepdims=True) for out in outs]
    ogs = [og_ref[rows, cols].astype(F32) for i, j, rows, cols in items]
    alongs = [jnp.mean(og * out, axis=-1, keepdims=True) for og, out in zip(ogs, outs)]
    factors = [lax.rsqrt(square + EPS) for square in squares]
    grads = []
    for out, factor, og, along, (i, j, rows, cols) in zip(outs, factors, ogs, alongs, items):
        normed = out * factor
        normed_ref[rows, cols] = normed.astype(BF16)
        grad = (factor * (og - (factor * along) * normed)).astype(BF16)
        grad_ref[i, rows, :] = grad
        grads.append(grad)
    parts = [t_dot(qd_ref[i, rows, :], grad) for grad, (i, j, rows, cols) in zip(grads, items)]
    totals = []
    for i in range(dims.per_step):
        total = parts[i * chunks + chunks - 1]
        for j in range(chunks - 2, -1, -1):
            suffix_ref[i, j] = total
            total = table_ref[i, j : j + 1, :] * total + parts[i * chunks + j]
        totals.append(total)
    split_store(dims, mine_ref, other_ref, totals)


def query_kernel(dims, core_ref, own, *rest):
    (
        k_ref, v_ref, grad_ref, run_ref, table_ref, weight_bias_ref, enter_bias_ref, prefix_ref, keep_ref, back_ref
    ) = own()
    dq_ref, dattend_ref = rest[-2:]
    chunks = dims.chunks
    items = items_of(chunks, dims.per_step)
    states = []
    for i, incoming in enumerate(split_load(dims, keep_ref, back_ref)):
        states += entering_states(chunks, i, incoming, table_ref, prefix_ref)
    grads = [grad_ref[i, rows, :] for i, j, rows, cols in items]
    scores = [dot_t(grad, v_ref[rows, cols]) for grad, (i, j, rows, cols) in zip(grads, items)]
    marks = [run_ref[i, :, rows] for i, j, rows, cols in items]
    runs = [columns(mark) for mark in marks]
    dattends = [
        (score * jnp.exp(run - mark + weight_bias_ref[rows, :])).astype(BF16)
        for score, run, mark, (i, j, rows, cols) in zip(scores, runs, marks, items)
    ]
    enters = [jnp.exp(run + enter_bias_ref[rows, :]) for run, (i, j, rows, cols) in zip(runs, items)]
    for x, (i, j, rows, cols) in enumerate(items):
        dattend_ref[i, rows, :] = dattends[x].T
        dq = dot(dattends[x], k_ref[rows, cols]) + enters[x] * dot_t(grads[x], states[x])
        dq_ref[rows, cols] = dq.astype(BF16)


def backward_kernel(dims, core_ref, own, *rest):
    (
        q_ref, grad_ref, attend_ref, dattend_ref, kd_ref, vd_ref, table_ref, suffix_ref, gkeep_ref, gback_ref
    ) = own()
    dk_ref, dv_ref = rest[-2:]
    chunks = dims.chunks
    items = items_of(chunks, dims.per_step)
    states = []
    for i, outgoing in enumerate(split_load(dims, gkeep_ref, gback_ref)):
        states += leaving_states(chunks, i, outgoing, table_ref, suffix_ref)
    for state, (i, j, rows, cols) in zip(states, items):
        dk = dot(dattend_ref[i, rows, :], q_ref[rows, cols]) + dot_t(vd_ref[i, rows, :], state)
        dk_ref[rows, cols] = dk.astype(BF16)
        dv = dot(attend_ref[i, rows, :], grad_ref[i, rows, :]) + dot(kd_ref[i, rows, :], state)
        dv_ref[rows, cols] = dv.astype(BF16)


def after(value, token):
    return value if token is None else lax.optimization_barrier((value, token))[0]


class Dims:
    def __init__(self, size, per_step, chunks, length, dh, heads):
        self.size, self.per_step, self.chunks = size, per_step, chunks
        self.length, self.dh, self.heads = length, dh, heads
        self.quarter = size // 2
        self.steps = size // per_step

    def head(self, group, p, core_ref):
        return (group + p // self.steps) * self.steps + lax.rem(p + core_ref[0] * (self.steps // 2), self.steps)

    def specs(self, group):
        n, halves = self.per_step, self.steps // 2
        length, dh, chunks = self.length, self.dh, self.chunks
        whole = lambda *shape: pl.BlockSpec(shape, lambda p, c: (0,) * len(shape))
        return dict(
            rows=pl.BlockSpec((length, n * dh), lambda p, c: (0, self.head(group, p, c))),
            run=pl.BlockSpec((n, 1, length), lambda p, c: (self.head(group, p, c), 0, 0)),
            table=pl.BlockSpec((n, 2 * chunks, C), lambda p, c: (self.head(group, p, c), 0, 0)),
            bias=whole(length, C),
            states=pl.BlockSpec((n, chunks - 1, dh, dh), lambda p, c: (p, 0, 0, 0)),
            headed=pl.BlockSpec((n, length, dh), lambda p, c: (p, 0, 0)),
            update=[
                pl.BlockSpec((n, dh, dh), lambda p, c, at=at: (jnp.clip(p - at * halves, 0, halves - 1), 0, 0))
                for at in range(2 * self.heads // self.size)
            ],
            mine=pl.BlockSpec((n, dh, dh), lambda p, c: (jnp.minimum(p, halves - 1), 0, 0)),
            other=pl.BlockSpec((n, dh, dh), lambda p, c: (jnp.maximum(p - halves, 0), 0, 0)),
            decay=whole(self.heads, length),
            start=whole(1, length),
            all_run=whole(self.heads, 1, length),
            all_table=whole(self.heads, 2 * chunks, C),
            all_gain=whole(self.heads, C),
            any=pl.BlockSpec(memory_space=pl.ANY),
        )


def with_rows(kernel, dims, group, which, inputs, core_ref, *refs):
    count = len(which)
    slots, sems = refs[len(refs) - 2 * count : len(refs) - count], refs[len(refs) - count :]
    refs = list(refs[: len(refs) - 2 * count])
    p = pl.program_id(0)
    width = dims.per_step * dims.dh

    def copy(x, step):
        start = pl.multiple_of(dims.head(group, step, core_ref) * width, width)
        return pltpu.make_async_copy(refs[which[x]].at[:, pl.ds(start, width)], slots[x].at[step], sems[x].at[step])

    @pl.when(p == 0)
    def _():
        for step in range(slots[0].shape[0]):
            for x in range(count):
                copy(x, step).start()

    def own():
        for x in range(count):
            copy(x, p).wait()
        return [slots[which.index(y)].at[p] if y in which else refs[y] for y in range(inputs)]

    own.plain = [refs[y] for y in range(inputs) if y not in which]
    kernel(dims, core_ref, own, *refs[inputs:])


def call_heads(
    dims, core_arg, kernel, group, in_names, out_names, out_shapes, args, name, products, reads, aliases=(), tokens=(),
    steps=None, stay=(),
):
    specs = dims.specs(group)
    steps = steps or dims.steps
    extra = [a for a in aliases if a is not None]
    which = [x for x, n in enumerate(in_names) if n == "rows"]
    args = [pltpu.with_memory_space_constraint(a, pltpu.HBM) if n in stay else a for n, a in zip(in_names, args)]
    in_specs = [pl.BlockSpec(memory_space=pltpu.HBM) if n == "rows" else specs[n] for n in in_names]
    return pl.pallas_call(
        functools.partial(with_rows, kernel, dims, group, which, len(in_names)),
        grid_spec=pltpu.PrefetchScalarGridSpec(
            num_scalar_prefetch=1,
            grid=(steps,),
            in_specs=in_specs + [specs["any"]] * (len(extra) + len(tokens)),
            out_specs=[s for n in out_names for s in (specs[n] if n == "update" else [specs[n]])],
            scratch_shapes=[pltpu.VMEM((steps, dims.length, dims.per_step * dims.dh), BF16) for _ in which]
            + [pltpu.SemaphoreType.DMA((steps,)) for _ in which],
        ),
        out_shape=out_shapes,
        input_output_aliases={1 + len(in_names) + i: i for i in range(len(extra))},
        compiler_params=pltpu.CompilerParams(
            dimension_semantics=("arbitrary",), vmem_limit_bytes=VMEM_LIMIT
        ),
        cost_estimate=pl.CostEstimate(
            flops=products * dims.size * 2 * dims.length * C * dims.dh,
            bytes_accessed=reads * dims.size * dims.length * dims.dh * 2,
            transcendentals=dims.size * dims.length * C,
        ),
        name=name,
    )(core_arg, *args, *extra, *tokens)


def local(query_in, key_in, value_in, log_decay, doc_start, out_grad):
    length, width = query_in.shape
    heads = log_decay.shape[0]
    dh = width // heads
    chunks = length // C
    groups = GROUPS
    size = heads // groups
    quarter = size // 2
    dims = Dims(size, min(PER_STEP, quarter), chunks, length, dh, heads)
    shards = lax.axis_size("seq")
    core = lax.axis_index("ctx")
    first = core == 0
    core_arg = core.astype(jnp.int32).reshape(1)
    swap = [(0, 1), (1, 0)]
    shape = jax.ShapeDtypeStruct
    states_shape = shape((size, chunks - 1, dh, dh), F32)
    part_shape = shape((quarter, dh, dh), F32)
    rows_shape = shape((length, width), BF16)
    bias_shape = shape((length, C), F32)
    call = functools.partial(call_heads, dims, core_arg)

    headed = lambda kind: shape((size, length, dh), kind)
    *updates, run, table, gain, weight_bias, enter_bias, leave_bias = call(
        begin_kernel, 0,
        ["decay", "start", "rows", "rows"],
        ["update", "all_run", "all_table", "all_gain", "bias", "bias", "bias"],
        (
            *[part_shape] * (2 * groups),
            shape((heads, 1, length), F32), shape((heads, 2 * chunks, C), F32), shape((heads, C), F32),
            bias_shape, bias_shape, bias_shape,
        ),
        (log_decay, doc_start.reshape(1, length), key_in, value_in),
        "begin", 1, 4,
        steps=groups * dims.steps,
        stay=("rows", "decay", "start"),
    )
    gain_other = lax.ppermute(gain, "ctx", swap)
    gain0 = jnp.where(first, gain, gain_other)
    gain1 = jnp.where(first, gain_other, gain)

    def pick(array, group):
        start = group * size + core * quarter
        return lax.dynamic_slice_in_dim(array, start, quarter, 0)[:, None, :]

    class Carry:
        def __init__(self, group, mine, other, backward):
            self.backward = backward
            self.g0, self.g1 = pick(gain0, group), pick(gain1, group)
            self.both = self.g0 * self.g1
            self.mine, self.got = mine, lax.ppermute(other, "ctx", swap)
            if backward:
                self.hops = [(k, k - 1) for k in range(shards - 1, 0, -1)]
            else:
                self.hops = [(k, k + 1) for k in range(shards - 1)]
            self.landed = []

        def start(self, token=None):
            got = after(self.got, token)
            self.zero = jnp.where(first, self.mine, got)
            self.one = jnp.where(first, got, self.mine)
            if self.backward:
                self.total = self.g0 * self.one + self.zero
            else:
                self.total = self.g1 * self.zero + self.one

        def hop(self, index, token=None):
            if index == 0:
                self.start(token)
                self.sent = self.total
            else:
                self.settle(token)
                self.sent = self.both * self.state + self.total
            self.landed.append(lax.ppermute(self.sent, "seq", [self.hops[index]]))

        def settle(self, token=None):
            self.landed[-1] = after(self.landed[-1], token)
            self.state = sum(self.landed[1:], self.landed[0])

        def finish(self, token=None):
            self.settle(token)
            state = self.state
            if self.backward:
                inner = self.g1 * state + self.one
                keep, send = jnp.where(first, inner, state), jnp.where(first, state, inner)
            else:
                inner = self.g0 * state + self.zero
                keep, send = jnp.where(first, state, inner), jnp.where(first, inner, state)
            return keep, lax.ppermute(send, "ctx", swap)

    def inside_of(group, token):
        return call(
            inside_kernel, group,
            ["rows"] * 3 + ["run", "table", "bias", "bias", "bias"],
            ["states"] + ["headed"] * 5,
            (states_shape, headed(F32), headed(BF16), headed(BF16), headed(BF16), headed(BF16)),
            (query_in, key_in, value_in, run, table, weight_bias, enter_bias, leave_bias),
            "inside", 4, 10,
            stay=("rows",),
            tokens=[token],
        )

    hops = range(shards - 1)
    carries = [Carry(group, updates[2 * group], updates[2 * group + 1], False) for group in range(groups)]
    insides = []
    token = None
    for index in hops:
        for carry in carries:
            carry.hop(index, token)
            token = carry.sent
        while index == min(1, shards - 2) and len(insides) < groups:
            insides.append(inside_of(len(insides), token))
            token = insides[-1][0]

    normed = None
    incoming, middles, backs = [], [], []
    for group in range(groups):
        incoming.append(carries[group].finish(token))
        prefix, inside, qd = insides[group][:3]
        normed, grad, suffix, mine, other = call(
            forward_kernel, group,
            ["headed", "headed", "rows", "table", "states", "mine", "other"],
            ["rows", "headed", "states", "mine", "other"],
            (rows_shape, headed(BF16), states_shape, part_shape, part_shape),
            (inside, qd, out_grad, table, prefix, *incoming[group]),
            "forward", 2, 8,
            aliases=(normed,),
            tokens=[backs[-1].sent] if backs else [],
        )
        token = mine
        middles.append((grad, suffix))
        backs.append(Carry(group, mine, other, True))
        if group == 0:
            backs[0].hop(0)

    query_gradient = None
    dattends = []

    def query_of(group, token):
        return call(
            query_kernel, group,
            ["rows", "rows", "headed", "run", "table", "bias", "bias", "states", "mine", "other"],
            ["rows", "headed"],
            (rows_shape, headed(BF16)),
            (
                key_in, value_in, middles[group][0], run, table, weight_bias, enter_bias, insides[group][0],
                *incoming[group],
            ),
            "query", 3, 8,
            aliases=(query_gradient,),
            tokens=[token],
        )

    for index in hops:
        for place, back in enumerate(backs):
            ahead = index + 1 if place == 0 else index
            if ahead in hops:
                back.hop(ahead, token)
                token = back.sent
        while index == min(1, shards - 2) and len(dattends) < groups:
            query_gradient, dattend = query_of(len(dattends), token)
            dattends.append(dattend)
            token = dattend
    grads = (None, None)
    for group in range(groups):
        grad, suffix = middles[group]
        kd, vd, attend = insides[group][3:]
        grads = call(
            backward_kernel, group,
            ["rows"] + ["headed"] * 5 + ["table", "states", "mine", "other"],
            ["rows", "rows"],
            (rows_shape, rows_shape),
            (query_in, grad, attend, dattends[group], kd, vd, table, suffix, *backs[group].finish(token)),
            "backward", 4, 10,
            aliases=grads,
        )
        token = grads[0]
    return (normed, query_gradient, *grads)


def solution(mesh):
    rows = P(("groups", "seq", "ctx"), "tensor")
    return jax.shard_map(
        local,
        mesh=mesh,
        in_specs=(rows, rows, rows, P("tensor", ("groups", "seq", "ctx")), P(("groups", "seq", "ctx")), rows),
        out_specs=(rows, rows, rows, rows),
        check_vma=False,
    )
```

```python
import functools

import jax
import jax.numpy as jnp
from jax import lax
from jax.experimental import pallas as pl
from jax.experimental.pallas import tpu as pltpu
from jax.sharding import PartitionSpec as P

C = 128
EPS = 1e-06
NEG = -1e30
GROUPS = 2
PER_STEP = 4
F32 = jnp.float32
BF16 = jnp.bfloat16
VMEM_LIMIT = 20 * 1024 * 1024


def dot(a, b):
    return lax.dot_general(a, b, (((1,), (0,)), ((), ())), preferred_element_type=F32)


def dot_t(a, b):
    return lax.dot_general(a, b, (((1,), (1,)), ((), ())), preferred_element_type=F32)


def t_dot(a, b):
    return lax.dot_general(a, b, (((0,), (0,)), ((), ())), preferred_element_type=F32)


def exact_dot(a, b):
    return lax.dot_general(
        a, b, (((1,), (0,)), ((), ())), precision=lax.Precision.HIGHEST, preferred_element_type=F32
    )


def columns(row):
    return jnp.broadcast_to(row, (C, C)).T


def fill_tables(chunks, decay_ref, start_ref, run_ref, table_ref, gain_ref, weight_bias_ref, enter_bias_ref, leave_bias_ref):
    heads = decay_ref.shape[0]
    at_row = lax.broadcasted_iota(jnp.int32, (C, C), 0)
    at_lane = lax.broadcasted_iota(jnp.int32, (C, C), 1)
    upper = jnp.where(at_row <= at_lane, 1.0, 0.0).astype(F32)
    sums = jnp.concatenate([upper, jnp.ones((C, C), F32)], axis=1)
    gain = jnp.ones((heads, C), F32)
    each = range(chunks)
    spans = [pl.ds(j * C, C) for j in each]
    runs = [exact_dot(decay_ref[:, span], sums) for span in spans]
    starts = jnp.concatenate([start_ref[:, span].astype(F32) for span in spans] * (8 // chunks), axis=0)
    docs_all = dot(starts.astype(BF16), sums.astype(BF16))
    for j in each:
        span = spans[j]
        last = runs[j][:, C:]
        docs, docs_last = docs_all[j : j + 1, :C], docs_all[j : j + 1, C:]
        passing = jnp.where(docs_last == 0.0, jnp.exp(last), 0.0)
        gain = gain * passing
        run_ref[:, 0, span] = runs[j][:, :C]
        table_ref[:, j, :] = passing
        table_ref[:, chunks + j, :] = last
        docs_column = columns(docs)
        weight_bias_ref[span, :] = jnp.where((docs_column == docs) & (at_lane <= at_row), 0.0, NEG)
        enter_bias_ref[span, :] = jnp.where(docs_column == 0.0, 0.0, NEG)
        leave_bias_ref[span, :] = jnp.where(docs_column == docs_last, 0.0, NEG)
    gain_ref[...] = gain


def items_of(chunks, per_step):
    return [(i, j, pl.ds(j * C, C), pl.ds(i * C, C)) for i in range(per_step) for j in range(chunks)]


def split_store(dims, mine_ref, other_ref, totals):
    mine = pl.program_id(0) * dims.per_step < dims.quarter

    @pl.when(mine)
    def _():
        for i, total in enumerate(totals):
            mine_ref[i] = total

    @pl.when(jnp.logical_not(mine))
    def _():
        for i, total in enumerate(totals):
            other_ref[i] = total


def split_load(dims, mine_ref, other_ref):
    mine = pl.program_id(0) * dims.per_step < dims.quarter
    return [jnp.where(mine, mine_ref[i], other_ref[i]) for i in range(dims.per_step)]


def leaving_decay(chunks, head, j, run, rows, table_ref, leave_bias_ref):
    return jnp.exp(table_ref[head, pl.ds(chunks + j, 1), :] - run + leave_bias_ref[rows, :])


def begin_kernel(dims, core_ref, own, *rest):
    updates_refs = rest[:-6]
    run_ref, table_ref, gain_ref, weight_bias_ref, enter_bias_ref, leave_bias_ref = rest[-6:]
    chunks = dims.chunks
    p = pl.program_id(0)

    @pl.when(p == 0)
    def _():
        fill_tables(
            chunks, *own.plain, run_ref, table_ref, gain_ref, weight_bias_ref, enter_bias_ref, leave_bias_ref
        )

    k_ref, v_ref = own()[2:]
    first = dims.head(0, p, core_ref) * dims.per_step
    items = items_of(chunks, dims.per_step)
    runs = [columns(run_ref[first + i, :, rows]) for i, j, rows, cols in items]
    leaves = [
        leaving_decay(chunks, first + i, j, run, rows, table_ref, leave_bias_ref)
        for run, (i, j, rows, cols) in zip(runs, items)
    ]
    kds = [(k_ref[rows, cols].astype(F32) * leave).astype(BF16) for leave, (i, j, rows, cols) in zip(leaves, items)]
    updates = [t_dot(kd, v_ref[rows, cols]) for kd, (i, j, rows, cols) in zip(kds, items)]
    totals = []
    for i in range(dims.per_step):
        total = updates[i * chunks]
        for j in range(1, chunks):
            total = table_ref[first + i, pl.ds(j, 1), :] * total + updates[i * chunks + j]
        totals.append(total)
    for at, ref in enumerate(updates_refs):

        @pl.when(p // (dims.steps // 2) == at)
        def _():
            for i, total in enumerate(totals):
                ref[i] = total


def inside_kernel(dims, core_ref, own, *rest):
    q_ref, k_ref, v_ref, run_ref, table_ref, weight_bias_ref, enter_bias_ref, leave_bias_ref = own()
    prefix_ref, inside_ref, qd_ref, kd_ref, vd_ref, attend_ref = rest[-6:]
    chunks = dims.chunks
    items = items_of(chunks, dims.per_step)
    q, k, v = ([ref[rows, cols] for i, j, rows, cols in items] for ref in (q_ref, k_ref, v_ref))
    scores = [dot_t(a, b) for a, b in zip(q, k)]
    marks = [run_ref[i, :, rows] for i, j, rows, cols in items]
    runs = [columns(mark) for mark in marks]
    leaves = [
        leaving_decay(chunks, i, j, run, rows, table_ref, leave_bias_ref)
        for run, (i, j, rows, cols) in zip(runs, items)
    ]
    kds = [(a.astype(F32) * leave).astype(BF16) for a, leave in zip(k, leaves)]
    attends = [
        (score * jnp.exp(run - mark + weight_bias_ref[rows, :])).astype(BF16)
        for score, run, mark, (i, j, rows, cols) in zip(scores, runs, marks, items)
    ]
    updates = [t_dot(kd, b) for kd, b in zip(kds, v)]
    for x, (i, j, rows, cols) in enumerate(items):
        inside_ref[i, rows, :] = dot(attends[x], v[x])
        attend_ref[i, rows, :] = attends[x].T
        kd_ref[i, rows, :] = kds[x]
        vd_ref[i, rows, :] = (v[x].astype(F32) * leaves[x]).astype(BF16)
        qd_ref[i, rows, :] = (q[x].astype(F32) * jnp.exp(runs[x] + enter_bias_ref[rows, :])).astype(BF16)
    for i in range(dims.per_step):
        total = None
        for j in range(chunks - 1):
            update = updates[i * chunks + j]
            total = update if total is None else table_ref[i, j : j + 1, :] * total + update
            prefix_ref[i, j] = total


def entering_states(chunks, i, incoming, table_ref, prefix_ref):
    states, gain = [], None
    for j in range(chunks):
        states.append((incoming if j == 0 else gain * incoming + prefix_ref[i, j - 1]).astype(BF16))
        passing = table_ref[i, j : j + 1, :]
        gain = passing if gain is None else gain * passing
    return states


def leaving_states(chunks, i, outgoing, table_ref, suffix_ref):
    states, gain = [None] * chunks, None
    for j in range(chunks - 1, -1, -1):
        states[j] = (outgoing if j == chunks - 1 else gain * outgoing + suffix_ref[i, j]).astype(BF16)
        passing = table_ref[i, j : j + 1, :]
        gain = passing if gain is None else gain * passing
    return states


def forward_kernel(dims, core_ref, own, *rest):
    inside_ref, qd_ref, og_ref, table_ref, prefix_ref, keep_ref, back_ref = own()
    normed_ref, grad_ref, suffix_ref, mine_ref, other_ref = rest[-5:]
    chunks = dims.chunks
    items = items_of(chunks, dims.per_step)
    states = []
    for i, incoming in enumerate(split_load(dims, keep_ref, back_ref)):
        states += entering_states(chunks, i, incoming, table_ref, prefix_ref)
    outs = [
        inside_ref[i, rows, :] + dot(qd_ref[i, rows, :], state) for state, (i, j, rows, cols) in zip(states, items)
    ]
    squares = [jnp.mean(out * out, axis=-1, keepdims=True) for out in outs]
    ogs = [og_ref[rows, cols].astype(F32) for i, j, rows, cols in items]
    alongs = [jnp.mean(og * out, axis=-1, keepdims=True) for og, out in zip(ogs, outs)]
    factors = [lax.rsqrt(square + EPS) for square in squares]
    grads = []
    for out, factor, og, along, (i, j, rows, cols) in zip(outs, factors, ogs, alongs, items):
        normed = out * factor
        normed_ref[rows, cols] = normed.astype(BF16)
        grad = (factor * (og - (factor * along) * normed)).astype(BF16)
        grad_ref[i, rows, :] = grad
        grads.append(grad)
    parts = [t_dot(qd_ref[i, rows, :], grad) for grad, (i, j, rows, cols) in zip(grads, items)]
    totals = []
    for i in range(dims.per_step):
        total = parts[i * chunks + chunks - 1]
        for j in range(chunks - 2, -1, -1):
            suffix_ref[i, j] = total
            total = table_ref[i, j : j + 1, :] * total + parts[i * chunks + j]
        totals.append(total)
    split_store(dims, mine_ref, other_ref, totals)


def query_kernel(dims, core_ref, own, *rest):
    (
        k_ref, v_ref, grad_ref, run_ref, table_ref, weight_bias_ref, enter_bias_ref, prefix_ref, keep_ref, back_ref
    ) = own()
    dq_ref, dattend_ref = rest[-2:]
    chunks = dims.chunks
    items = items_of(chunks, dims.per_step)
    states = []
    for i, incoming in enumerate(split_load(dims, keep_ref, back_ref)):
        states += entering_states(chunks, i, incoming, table_ref, prefix_ref)
    grads = [grad_ref[i, rows, :] for i, j, rows, cols in items]
    scores = [dot_t(grad, v_ref[rows, cols]) for grad, (i, j, rows, cols) in zip(grads, items)]
    marks = [run_ref[i, :, rows] for i, j, rows, cols in items]
    runs = [columns(mark) for mark in marks]
    dattends = [
        (score * jnp.exp(run - mark + weight_bias_ref[rows, :])).astype(BF16)
        for score, run, mark, (i, j, rows, cols) in zip(scores, runs, marks, items)
    ]
    enters = [jnp.exp(run + enter_bias_ref[rows, :]) for run, (i, j, rows, cols) in zip(runs, items)]
    for x, (i, j, rows, cols) in enumerate(items):
        dattend_ref[i, rows, :] = dattends[x].T
        dq = dot(dattends[x], k_ref[rows, cols]) + enters[x] * dot_t(grads[x], states[x])
        dq_ref[rows, cols] = dq.astype(BF16)


def backward_kernel(dims, core_ref, own, *rest):
    (
        q_ref, grad_ref, attend_ref, dattend_ref, kd_ref, vd_ref, table_ref, suffix_ref, gkeep_ref, gback_ref
    ) = own()
    dk_ref, dv_ref = rest[-2:]
    chunks = dims.chunks
    items = items_of(chunks, dims.per_step)
    states = []
    for i, outgoing in enumerate(split_load(dims, gkeep_ref, gback_ref)):
        states += leaving_states(chunks, i, outgoing, table_ref, suffix_ref)
    for state, (i, j, rows, cols) in zip(states, items):
        dk = dot(dattend_ref[i, rows, :], q_ref[rows, cols]) + dot_t(vd_ref[i, rows, :], state)
        dk_ref[rows, cols] = dk.astype(BF16)
        dv = dot(attend_ref[i, rows, :], grad_ref[i, rows, :]) + dot(kd_ref[i, rows, :], state)
        dv_ref[rows, cols] = dv.astype(BF16)


def after(value, token):
    return value if token is None else lax.optimization_barrier((value, token))[0]


class Dims:
    def __init__(self, size, per_step, chunks, length, dh, heads):
        self.size, self.per_step, self.chunks = size, per_step, chunks
        self.length, self.dh, self.heads = length, dh, heads
        self.quarter = size // 2
        self.steps = size // per_step

    def head(self, group, p, core_ref):
        return (group + p // self.steps) * self.steps + lax.rem(p + core_ref[0] * (self.steps // 2), self.steps)

    def specs(self, group):
        n, halves = self.per_step, self.steps // 2
        length, dh, chunks = self.length, self.dh, self.chunks
        whole = lambda *shape: pl.BlockSpec(shape, lambda p, c: (0,) * len(shape))
        return dict(
            rows=pl.BlockSpec((length, n * dh), lambda p, c: (0, self.head(group, p, c))),
            run=pl.BlockSpec((n, 1, length), lambda p, c: (self.head(group, p, c), 0, 0)),
            table=pl.BlockSpec((n, 2 * chunks, C), lambda p, c: (self.head(group, p, c), 0, 0)),
            bias=whole(length, C),
            states=pl.BlockSpec((n, chunks - 1, dh, dh), lambda p, c: (p, 0, 0, 0)),
            headed=pl.BlockSpec((n, length, dh), lambda p, c: (p, 0, 0)),
            update=[
                pl.BlockSpec((n, dh, dh), lambda p, c, at=at: (jnp.clip(p - at * halves, 0, halves - 1), 0, 0))
                for at in range(2 * self.heads // self.size)
            ],
            mine=pl.BlockSpec((n, dh, dh), lambda p, c: (jnp.minimum(p, halves - 1), 0, 0)),
            other=pl.BlockSpec((n, dh, dh), lambda p, c: (jnp.maximum(p - halves, 0), 0, 0)),
            decay=whole(self.heads, length),
            start=whole(1, length),
            all_run=whole(self.heads, 1, length),
            all_table=whole(self.heads, 2 * chunks, C),
            all_gain=whole(self.heads, C),
            any=pl.BlockSpec(memory_space=pl.ANY),
        )


def with_rows(kernel, dims, group, which, inputs, core_ref, *refs):
    count = len(which)
    slots, sems = refs[len(refs) - 2 * count : len(refs) - count], refs[len(refs) - count :]
    refs = list(refs[: len(refs) - 2 * count])
    p = pl.program_id(0)
    width = dims.per_step * dims.dh

    def copy(x, step):
        start = pl.multiple_of(dims.head(group, step, core_ref) * width, width)
        return pltpu.make_async_copy(refs[which[x]].at[:, pl.ds(start, width)], slots[x].at[step], sems[x].at[step])

    @pl.when(p == 0)
    def _():
        for step in range(slots[0].shape[0]):
            for x in range(count):
                copy(x, step).start()

    def own():
        for x in range(count):
            copy(x, p).wait()
        return [slots[which.index(y)].at[p] if y in which else refs[y] for y in range(inputs)]

    own.plain = [refs[y] for y in range(inputs) if y not in which]
    kernel(dims, core_ref, own, *refs[inputs:])


def call_heads(
    dims, core_arg, kernel, group, in_names, out_names, out_shapes, args, name, products, reads, aliases=(), tokens=(),
    steps=None, stay=(),
):
    specs = dims.specs(group)
    steps = steps or dims.steps
    extra = [a for a in aliases if a is not None]
    which = [x for x, n in enumerate(in_names) if n == "rows"]
    args = [pltpu.with_memory_space_constraint(a, pltpu.HBM) if n in stay else a for n, a in zip(in_names, args)]
    in_specs = [pl.BlockSpec(memory_space=pltpu.HBM) if n == "rows" else specs[n] for n in in_names]
    return pl.pallas_call(
        functools.partial(with_rows, kernel, dims, group, which, len(in_names)),
        grid_spec=pltpu.PrefetchScalarGridSpec(
            num_scalar_prefetch=1,
            grid=(steps,),
            in_specs=in_specs + [specs["any"]] * (len(extra) + len(tokens)),
            out_specs=[s for n in out_names for s in (specs[n] if n == "update" else [specs[n]])],
            scratch_shapes=[pltpu.VMEM((steps, dims.length, dims.per_step * dims.dh), BF16) for _ in which]
            + [pltpu.SemaphoreType.DMA((steps,)) for _ in which],
        ),
        out_shape=out_shapes,
        input_output_aliases={1 + len(in_names) + i: i for i in range(len(extra))},
        compiler_params=pltpu.CompilerParams(
            dimension_semantics=("arbitrary",), vmem_limit_bytes=VMEM_LIMIT
        ),
        cost_estimate=pl.CostEstimate(
            flops=products * dims.size * 2 * dims.length * C * dims.dh,
            bytes_accessed=reads * dims.size * dims.length * dims.dh * 2,
            transcendentals=dims.size * dims.length * C,
        ),
        name=name,
    )(core_arg, *args, *extra, *tokens)


def local(query_in, key_in, value_in, log_decay, doc_start, out_grad):
    length, width = query_in.shape
    heads = log_decay.shape[0]
    dh = width // heads
    chunks = length // C
    groups = GROUPS
    size = heads // groups
    quarter = size // 2
    dims = Dims(size, min(PER_STEP, quarter), chunks, length, dh, heads)
    shards = lax.axis_size("seq")
    core = lax.axis_index("ctx")
    first = core == 0
    core_arg = core.astype(jnp.int32).reshape(1)
    swap = [(0, 1), (1, 0)]
    shape = jax.ShapeDtypeStruct
    states_shape = shape((size, chunks - 1, dh, dh), F32)
    part_shape = shape((quarter, dh, dh), F32)
    rows_shape = shape((length, width), BF16)
    bias_shape = shape((length, C), F32)
    call = functools.partial(call_heads, dims, core_arg)

    headed = lambda kind: shape((size, length, dh), kind)
    *updates, run, table, gain, weight_bias, enter_bias, leave_bias = call(
        begin_kernel, 0,
        ["decay", "start", "rows", "rows"],
        ["update", "all_run", "all_table", "all_gain", "bias", "bias", "bias"],
        (
            *[part_shape] * (2 * groups),
            shape((heads, 1, length), F32), shape((heads, 2 * chunks, C), F32), shape((heads, C), F32),
            bias_shape, bias_shape, bias_shape,
        ),
        (log_decay, doc_start.reshape(1, length), key_in, value_in),
        "begin", 1, 4,
        steps=groups * dims.steps,
        stay=("rows", "decay", "start"),
    )
    gain_other = lax.ppermute(gain, "ctx", swap)
    gain0 = jnp.where(first, gain, gain_other)
    gain1 = jnp.where(first, gain_other, gain)

    def pick(array, group):
        start = group * size + core * quarter
        return lax.dynamic_slice_in_dim(array, start, quarter, 0)[:, None, :]

    class Carry:
        def __init__(self, group, mine, other, backward):
            self.backward = backward
            self.g0, self.g1 = pick(gain0, group), pick(gain1, group)
            self.both = self.g0 * self.g1
            self.mine, self.got = mine, lax.ppermute(other, "ctx", swap)
            if backward:
                self.hops = [(k, k - 1) for k in range(shards - 1, 0, -1)]
            else:
                self.hops = [(k, k + 1) for k in range(shards - 1)]
            self.landed = []

        def start(self, token=None):
            got = after(self.got, token)
            self.zero = jnp.where(first, self.mine, got)
            self.one = jnp.where(first, got, self.mine)
            if self.backward:
                self.total = self.g0 * self.one + self.zero
            else:
                self.total = self.g1 * self.zero + self.one

        def hop(self, index, token=None):
            if index == 0:
                self.start(token)
                self.sent = self.total
            else:
                self.settle(token)
                self.sent = self.both * self.state + self.total
            self.landed.append(lax.ppermute(self.sent, "seq", [self.hops[index]]))

        def settle(self, token=None):
            self.landed[-1] = after(self.landed[-1], token)
            self.state = sum(self.landed[1:], self.landed[0])

        def finish(self, token=None):
            self.settle(token)
            state = self.state
            if self.backward:
                inner = self.g1 * state + self.one
                keep, send = jnp.where(first, inner, state), jnp.where(first, state, inner)
            else:
                inner = self.g0 * state + self.zero
                keep, send = jnp.where(first, state, inner), jnp.where(first, inner, state)
            return keep, lax.ppermute(send, "ctx", swap)

    def inside_of(group, token):
        return call(
            inside_kernel, group,
            ["rows"] * 3 + ["run", "table", "bias", "bias", "bias"],
            ["states"] + ["headed"] * 5,
            (states_shape, headed(F32), headed(BF16), headed(BF16), headed(BF16), headed(BF16)),
            (query_in, key_in, value_in, run, table, weight_bias, enter_bias, leave_bias),
            "inside", 4, 10,
            stay=("rows",),
            tokens=[token],
        )

    hops = range(shards - 1)
    carries = [Carry(group, updates[2 * group], updates[2 * group + 1], False) for group in range(groups)]
    insides = []
    token = None
    for index in hops:
        for carry in carries:
            carry.hop(index, token)
            token = carry.sent
        while index == min(1, shards - 2) and len(insides) < groups:
            insides.append(inside_of(len(insides), token))
            token = insides[-1][0]

    normed = None
    incoming, middles, backs = [], [], []
    query_gradient = None
    dattends = []

    def query_of(group, token):
        return call(
            query_kernel, group,
            ["rows", "rows", "headed", "run", "table", "bias", "bias", "states", "mine", "other"],
            ["rows", "headed"],
            (rows_shape, headed(BF16)),
            (
                key_in, value_in, middles[group][0], run, table, weight_bias, enter_bias, insides[group][0],
                *incoming[group],
            ),
            "query", 3, 8,
            aliases=(query_gradient,),
            tokens=[token],
        )

    for group in range(groups):
        incoming.append(carries[group].finish(token))
        prefix, inside, qd = insides[group][:3]
        normed, grad, suffix, mine, other = call(
            forward_kernel, group,
            ["headed", "headed", "rows", "table", "states", "mine", "other"],
            ["rows", "headed", "states", "mine", "other"],
            (rows_shape, headed(BF16), states_shape, part_shape, part_shape),
            (inside, qd, out_grad, table, prefix, *incoming[group]),
            "forward", 2, 8,
            aliases=(normed,),
            tokens=[backs[-1].sent] if backs else [],
        )
        token = mine
        middles.append((grad, suffix))
        backs.append(Carry(group, mine, other, True))
        if group < groups - 1:
            query_gradient, dattend = query_of(group, token)
            dattends.append(dattend)
            token = dattend
        if group == 0:
            backs[0].hop(0)

    for index in hops:
        for place, back in enumerate(backs):
            ahead = index + 1 if place == 0 else index
            if ahead in hops:
                back.hop(ahead, token)
                token = back.sent
        while index == min(1, shards - 2) and len(dattends) < groups:
            query_gradient, dattend = query_of(len(dattends), token)
            dattends.append(dattend)
            token = dattend
    grads = (None, None)
    for group in range(groups):
        grad, suffix = middles[group]
        kd, vd, attend = insides[group][3:]
        grads = call(
            backward_kernel, group,
            ["rows"] + ["headed"] * 5 + ["table", "states", "mine", "other"],
            ["rows", "rows"],
            (rows_shape, rows_shape),
            (query_in, grad, attend, dattends[group], kd, vd, table, suffix, *backs[group].finish(token)),
            "backward", 4, 10,
            aliases=grads,
        )
        token = grads[0]
    return (normed, query_gradient, *grads)


def solution(mesh):
    rows = P(("groups", "seq", "ctx"), "tensor")
    return jax.shard_map(
        local,
        mesh=mesh,
        in_specs=(rows, rows, rows, P("tensor", ("groups", "seq", "ctx")), P(("groups", "seq", "ctx")), rows),
        out_specs=(rows, rows, rows, rows),
        check_vma=False,
    )
```

```python
import functools

import jax
import jax.numpy as jnp
from jax import lax
from jax.experimental import pallas as pl
from jax.experimental.pallas import tpu as pltpu
from jax.sharding import PartitionSpec as P

C = 128
EPS = 1e-06
NEG = -1e30
GROUPS = 2
PER_STEP = 4
F32 = jnp.float32
BF16 = jnp.bfloat16
VMEM_LIMIT = 20 * 1024 * 1024


def dot(a, b):
    return lax.dot_general(a, b, (((1,), (0,)), ((), ())), preferred_element_type=F32)


def dot_t(a, b):
    return lax.dot_general(a, b, (((1,), (1,)), ((), ())), preferred_element_type=F32)


def t_dot(a, b):
    return lax.dot_general(a, b, (((0,), (0,)), ((), ())), preferred_element_type=F32)


def exact_dot(a, b):
    return lax.dot_general(
        a, b, (((1,), (0,)), ((), ())), precision=lax.Precision.HIGHEST, preferred_element_type=F32
    )


def columns(row):
    return jnp.broadcast_to(row, (C, C)).T


def fill_tables(chunks, decay_ref, start_ref, run_ref, table_ref, gain_ref, weight_bias_ref, enter_bias_ref, leave_bias_ref):
    heads = decay_ref.shape[0]
    at_row = lax.broadcasted_iota(jnp.int32, (C, C), 0)
    at_lane = lax.broadcasted_iota(jnp.int32, (C, C), 1)
    upper = jnp.where(at_row <= at_lane, 1.0, 0.0).astype(F32)
    sums = jnp.concatenate([upper, jnp.ones((C, C), F32)], axis=1)
    gain = jnp.ones((heads, C), F32)
    each = range(chunks)
    spans = [pl.ds(j * C, C) for j in each]
    runs = [exact_dot(decay_ref[:, span], upper) for span in spans]
    starts = jnp.concatenate([start_ref[:, span].astype(F32) for span in spans] * (8 // chunks), axis=0)
    docs_all = dot(starts.astype(BF16), sums.astype(BF16))
    for j in each:
        span = spans[j]
        last = jnp.broadcast_to(runs[j][:, C - 1 :], (heads, C))
        docs, docs_last = docs_all[j : j + 1, :C], docs_all[j : j + 1, C:]
        passing = jnp.where(docs_last == 0.0, jnp.exp(last), 0.0)
        gain = gain * passing
        run_ref[:, 0, span] = runs[j]
        table_ref[:, j, :] = passing
        table_ref[:, chunks + j, :] = last
        docs_column = columns(docs)
        weight_bias_ref[span, :] = jnp.where((docs_column == docs) & (at_lane <= at_row), 0.0, NEG)
        enter_bias_ref[span, :] = jnp.where(docs_column == 0.0, 0.0, NEG)
        leave_bias_ref[span, :] = jnp.where(docs_column == docs_last, 0.0, NEG)
    gain_ref[...] = gain


def items_of(chunks, per_step):
    return [(i, j, pl.ds(j * C, C), pl.ds(i * C, C)) for i in range(per_step) for j in range(chunks)]


def split_store(dims, mine_ref, other_ref, totals):
    mine = pl.program_id(0) * dims.per_step < dims.quarter

    @pl.when(mine)
    def _():
        for i, total in enumerate(totals):
            mine_ref[i] = total

    @pl.when(jnp.logical_not(mine))
    def _():
        for i, total in enumerate(totals):
            other_ref[i] = total


def split_load(dims, mine_ref, other_ref):
    mine = pl.program_id(0) * dims.per_step < dims.quarter
    return [jnp.where(mine, mine_ref[i], other_ref[i]) for i in range(dims.per_step)]


def leaving_decay(chunks, head, j, run, rows, table_ref, leave_bias_ref):
    return jnp.exp(table_ref[head, pl.ds(chunks + j, 1), :] - run + leave_bias_ref[rows, :])


def begin_kernel(dims, core_ref, own, *rest):
    updates_refs = rest[:-6]
    run_ref, table_ref, gain_ref, weight_bias_ref, enter_bias_ref, leave_bias_ref = rest[-6:]
    chunks = dims.chunks
    p = pl.program_id(0)

    @pl.when(p == 0)
    def _():
        fill_tables(
            chunks, *own.plain, run_ref, table_ref, gain_ref, weight_bias_ref, enter_bias_ref, leave_bias_ref
        )

    k_ref, v_ref = own()[2:]
    first = dims.head(0, p, core_ref) * dims.per_step
    items = items_of(chunks, dims.per_step)
    runs = [columns(run_ref[first + i, :, rows]) for i, j, rows, cols in items]
    leaves = [
        leaving_decay(chunks, first + i, j, run, rows, table_ref, leave_bias_ref)
        for run, (i, j, rows, cols) in zip(runs, items)
    ]
    kds = [(k_ref[rows, cols].astype(F32) * leave).astype(BF16) for leave, (i, j, rows, cols) in zip(leaves, items)]
    updates = [t_dot(kd, v_ref[rows, cols]) for kd, (i, j, rows, cols) in zip(kds, items)]
    totals = []
    for i in range(dims.per_step):
        total = updates[i * chunks]
        for j in range(1, chunks):
            total = table_ref[first + i, pl.ds(j, 1), :] * total + updates[i * chunks + j]
        totals.append(total)
    for at, ref in enumerate(updates_refs):

        @pl.when(p // (dims.steps // 2) == at)
        def _():
            for i, total in enumerate(totals):
                ref[i] = total


def inside_kernel(dims, core_ref, own, *rest):
    q_ref, k_ref, v_ref, run_ref, table_ref, weight_bias_ref, enter_bias_ref, leave_bias_ref = own()
    prefix_ref, inside_ref, qd_ref, kd_ref, vd_ref, attend_ref = rest[-6:]
    chunks = dims.chunks
    items = items_of(chunks, dims.per_step)
    q, k, v = ([ref[rows, cols] for i, j, rows, cols in items] for ref in (q_ref, k_ref, v_ref))
    scores = [dot_t(a, b) for a, b in zip(q, k)]
    marks = [run_ref[i, :, rows] for i, j, rows, cols in items]
    runs = [columns(mark) for mark in marks]
    leaves = [
        leaving_decay(chunks, i, j, run, rows, table_ref, leave_bias_ref)
        for run, (i, j, rows, cols) in zip(runs, items)
    ]
    kds = [(a.astype(F32) * leave).astype(BF16) for a, leave in zip(k, leaves)]
    attends = [
        (score * jnp.exp(run - mark + weight_bias_ref[rows, :])).astype(BF16)
        for score, run, mark, (i, j, rows, cols) in zip(scores, runs, marks, items)
    ]
    updates = [t_dot(kd, b) for kd, b in zip(kds, v)]
    for x, (i, j, rows, cols) in enumerate(items):
        inside_ref[i, rows, :] = dot(attends[x], v[x])
        attend_ref[i, rows, :] = attends[x].T
        kd_ref[i, rows, :] = kds[x]
        vd_ref[i, rows, :] = (v[x].astype(F32) * leaves[x]).astype(BF16)
        qd_ref[i, rows, :] = (q[x].astype(F32) * jnp.exp(runs[x] + enter_bias_ref[rows, :])).astype(BF16)
    for i in range(dims.per_step):
        total = None
        for j in range(chunks - 1):
            update = updates[i * chunks + j]
            total = update if total is None else table_ref[i, j : j + 1, :] * total + update
            prefix_ref[i, j] = total


def entering_states(chunks, i, incoming, table_ref, prefix_ref):
    states, gain = [], None
    for j in range(chunks):
        states.append((incoming if j == 0 else gain * incoming + prefix_ref[i, j - 1]).astype(BF16))
        passing = table_ref[i, j : j + 1, :]
        gain = passing if gain is None else gain * passing
    return states


def leaving_states(chunks, i, outgoing, table_ref, suffix_ref):
    states, gain = [None] * chunks, None
    for j in range(chunks - 1, -1, -1):
        states[j] = (outgoing if j == chunks - 1 else gain * outgoing + suffix_ref[i, j]).astype(BF16)
        passing = table_ref[i, j : j + 1, :]
        gain = passing if gain is None else gain * passing
    return states


def forward_kernel(dims, core_ref, own, *rest):
    inside_ref, qd_ref, og_ref, table_ref, prefix_ref, keep_ref, back_ref = own()
    normed_ref, grad_ref, suffix_ref, mine_ref, other_ref = rest[-5:]
    chunks = dims.chunks
    items = items_of(chunks, dims.per_step)
    states = []
    for i, incoming in enumerate(split_load(dims, keep_ref, back_ref)):
        states += entering_states(chunks, i, incoming, table_ref, prefix_ref)
    outs = [
        inside_ref[i, rows, :] + dot(qd_ref[i, rows, :], state) for state, (i, j, rows, cols) in zip(states, items)
    ]
    squares = [jnp.mean(out * out, axis=-1, keepdims=True) for out in outs]
    ogs = [og_ref[rows, cols].astype(F32) for i, j, rows, cols in items]
    alongs = [jnp.mean(og * out, axis=-1, keepdims=True) for og, out in zip(ogs, outs)]
    factors = [lax.rsqrt(square + EPS) for square in squares]
    grads = []
    for out, factor, og, along, (i, j, rows, cols) in zip(outs, factors, ogs, alongs, items):
        normed = out * factor
        normed_ref[rows, cols] = normed.astype(BF16)
        grad = (factor * (og - (factor * along) * normed)).astype(BF16)
        grad_ref[i, rows, :] = grad
        grads.append(grad)
    parts = [t_dot(qd_ref[i, rows, :], grad) for grad, (i, j, rows, cols) in zip(grads, items)]
    totals = []
    for i in range(dims.per_step):
        total = parts[i * chunks + chunks - 1]
        for j in range(chunks - 2, -1, -1):
            suffix_ref[i, j] = total
            total = table_ref[i, j : j + 1, :] * total + parts[i * chunks + j]
        totals.append(total)
    split_store(dims, mine_ref, other_ref, totals)


def query_kernel(dims, core_ref, own, *rest):
    (
        k_ref, v_ref, grad_ref, run_ref, table_ref, weight_bias_ref, enter_bias_ref, prefix_ref, keep_ref, back_ref
    ) = own()
    dq_ref, dattend_ref = rest[-2:]
    chunks = dims.chunks
    items = items_of(chunks, dims.per_step)
    states = []
    for i, incoming in enumerate(split_load(dims, keep_ref, back_ref)):
        states += entering_states(chunks, i, incoming, table_ref, prefix_ref)
    grads = [grad_ref[i, rows, :] for i, j, rows, cols in items]
    scores = [dot_t(grad, v_ref[rows, cols]) for grad, (i, j, rows, cols) in zip(grads, items)]
    marks = [run_ref[i, :, rows] for i, j, rows, cols in items]
    runs = [columns(mark) for mark in marks]
    dattends = [
        (score * jnp.exp(run - mark + weight_bias_ref[rows, :])).astype(BF16)
        for score, run, mark, (i, j, rows, cols) in zip(scores, runs, marks, items)
    ]
    enters = [jnp.exp(run + enter_bias_ref[rows, :]) for run, (i, j, rows, cols) in zip(runs, items)]
    for x, (i, j, rows, cols) in enumerate(items):
        dattend_ref[i, rows, :] = dattends[x].T
        dq = dot(dattends[x], k_ref[rows, cols]) + enters[x] * dot_t(grads[x], states[x])
        dq_ref[rows, cols] = dq.astype(BF16)


def backward_kernel(dims, core_ref, own, *rest):
    (
        q_ref, grad_ref, attend_ref, dattend_ref, kd_ref, vd_ref, table_ref, suffix_ref, gkeep_ref, gback_ref
    ) = own()
    dk_ref, dv_ref = rest[-2:]
    chunks = dims.chunks
    items = items_of(chunks, dims.per_step)
    states = []
    for i, outgoing in enumerate(split_load(dims, gkeep_ref, gback_ref)):
        states += leaving_states(chunks, i, outgoing, table_ref, suffix_ref)
    for state, (i, j, rows, cols) in zip(states, items):
        dk = dot(dattend_ref[i, rows, :], q_ref[rows, cols]) + dot_t(vd_ref[i, rows, :], state)
        dk_ref[rows, cols] = dk.astype(BF16)
        dv = dot(attend_ref[i, rows, :], grad_ref[i, rows, :]) + dot(kd_ref[i, rows, :], state)
        dv_ref[rows, cols] = dv.astype(BF16)


def after(value, token):
    return value if token is None else lax.optimization_barrier((value, token))[0]


class Dims:
    def __init__(self, size, per_step, chunks, length, dh, heads):
        self.size, self.per_step, self.chunks = size, per_step, chunks
        self.length, self.dh, self.heads = length, dh, heads
        self.quarter = size // 2
        self.steps = size // per_step

    def head(self, group, p, core_ref):
        return (group + p // self.steps) * self.steps + lax.rem(p + core_ref[0] * (self.steps // 2), self.steps)

    def specs(self, group):
        n, halves = self.per_step, self.steps // 2
        length, dh, chunks = self.length, self.dh, self.chunks
        whole = lambda *shape: pl.BlockSpec(shape, lambda p, c: (0,) * len(shape))
        return dict(
            rows=pl.BlockSpec((length, n * dh), lambda p, c: (0, self.head(group, p, c))),
            run=pl.BlockSpec((n, 1, length), lambda p, c: (self.head(group, p, c), 0, 0)),
            table=pl.BlockSpec((n, 2 * chunks, C), lambda p, c: (self.head(group, p, c), 0, 0)),
            bias=whole(length, C),
            states=pl.BlockSpec((n, chunks - 1, dh, dh), lambda p, c: (p, 0, 0, 0)),
            headed=pl.BlockSpec((n, length, dh), lambda p, c: (p, 0, 0)),
            update=[
                pl.BlockSpec((n, dh, dh), lambda p, c, at=at: (jnp.clip(p - at * halves, 0, halves - 1), 0, 0))
                for at in range(2 * self.heads // self.size)
            ],
            mine=pl.BlockSpec((n, dh, dh), lambda p, c: (jnp.minimum(p, halves - 1), 0, 0)),
            other=pl.BlockSpec((n, dh, dh), lambda p, c: (jnp.maximum(p - halves, 0), 0, 0)),
            decay=whole(self.heads, length),
            start=whole(1, length),
            all_run=whole(self.heads, 1, length),
            all_table=whole(self.heads, 2 * chunks, C),
            all_gain=whole(self.heads, C),
            any=pl.BlockSpec(memory_space=pl.ANY),
        )


def with_rows(kernel, dims, group, which, inputs, core_ref, *refs):
    count = len(which)
    slots, sems = refs[len(refs) - 2 * count : len(refs) - count], refs[len(refs) - count :]
    refs = list(refs[: len(refs) - 2 * count])
    p = pl.program_id(0)
    width = dims.per_step * dims.dh

    def copy(x, step):
        start = pl.multiple_of(dims.head(group, step, core_ref) * width, width)
        return pltpu.make_async_copy(refs[which[x]].at[:, pl.ds(start, width)], slots[x].at[step], sems[x].at[step])

    @pl.when(p == 0)
    def _():
        for step in range(slots[0].shape[0]):
            for x in range(count):
                copy(x, step).start()

    def own():
        for x in range(count):
            copy(x, p).wait()
        return [slots[which.index(y)].at[p] if y in which else refs[y] for y in range(inputs)]

    own.plain = [refs[y] for y in range(inputs) if y not in which]
    kernel(dims, core_ref, own, *refs[inputs:])


def call_heads(
    dims, core_arg, kernel, group, in_names, out_names, out_shapes, args, name, products, reads, aliases=(), tokens=(),
    steps=None, stay=(),
):
    specs = dims.specs(group)
    steps = steps or dims.steps
    extra = [a for a in aliases if a is not None]
    which = [x for x, n in enumerate(in_names) if n == "rows"]
    args = [pltpu.with_memory_space_constraint(a, pltpu.HBM) if n in stay else a for n, a in zip(in_names, args)]
    in_specs = [pl.BlockSpec(memory_space=pltpu.HBM) if n == "rows" else specs[n] for n in in_names]
    return pl.pallas_call(
        functools.partial(with_rows, kernel, dims, group, which, len(in_names)),
        grid_spec=pltpu.PrefetchScalarGridSpec(
            num_scalar_prefetch=1,
            grid=(steps,),
            in_specs=in_specs + [specs["any"]] * (len(extra) + len(tokens)),
            out_specs=[s for n in out_names for s in (specs[n] if n == "update" else [specs[n]])],
            scratch_shapes=[pltpu.VMEM((steps, dims.length, dims.per_step * dims.dh), BF16) for _ in which]
            + [pltpu.SemaphoreType.DMA((steps,)) for _ in which],
        ),
        out_shape=out_shapes,
        input_output_aliases={1 + len(in_names) + i: i for i in range(len(extra))},
        compiler_params=pltpu.CompilerParams(
            dimension_semantics=("arbitrary",), vmem_limit_bytes=VMEM_LIMIT
        ),
        cost_estimate=pl.CostEstimate(
            flops=products * dims.size * 2 * dims.length * C * dims.dh,
            bytes_accessed=reads * dims.size * dims.length * dims.dh * 2,
            transcendentals=dims.size * dims.length * C,
        ),
        name=name,
    )(core_arg, *args, *extra, *tokens)


def local(query_in, key_in, value_in, log_decay, doc_start, out_grad):
    length, width = query_in.shape
    heads = log_decay.shape[0]
    dh = width // heads
    chunks = length // C
    groups = GROUPS
    size = heads // groups
    quarter = size // 2
    dims = Dims(size, min(PER_STEP, quarter), chunks, length, dh, heads)
    shards = lax.axis_size("seq")
    core = lax.axis_index("ctx")
    first = core == 0
    core_arg = core.astype(jnp.int32).reshape(1)
    swap = [(0, 1), (1, 0)]
    shape = jax.ShapeDtypeStruct
    states_shape = shape((size, chunks - 1, dh, dh), F32)
    part_shape = shape((quarter, dh, dh), F32)
    rows_shape = shape((length, width), BF16)
    bias_shape = shape((length, C), F32)
    call = functools.partial(call_heads, dims, core_arg)

    headed = lambda kind: shape((size, length, dh), kind)
    *updates, run, table, gain, weight_bias, enter_bias, leave_bias = call(
        begin_kernel, 0,
        ["decay", "start", "rows", "rows"],
        ["update", "all_run", "all_table", "all_gain", "bias", "bias", "bias"],
        (
            *[part_shape] * (2 * groups),
            shape((heads, 1, length), F32), shape((heads, 2 * chunks, C), F32), shape((heads, C), F32),
            bias_shape, bias_shape, bias_shape,
        ),
        (log_decay, doc_start.reshape(1, length), key_in, value_in),
        "begin", 1, 4,
        steps=groups * dims.steps,
        stay=("rows", "decay", "start"),
    )
    gain_other = lax.ppermute(gain, "ctx", swap)
    gain0 = jnp.where(first, gain, gain_other)
    gain1 = jnp.where(first, gain_other, gain)

    def pick(array, group):
        start = group * size + core * quarter
        return lax.dynamic_slice_in_dim(array, start, quarter, 0)[:, None, :]

    class Carry:
        def __init__(self, group, mine, other, backward):
            self.backward = backward
            self.g0, self.g1 = pick(gain0, group), pick(gain1, group)
            self.both = self.g0 * self.g1
            self.mine, self.got = mine, lax.ppermute(other, "ctx", swap)
            if backward:
                self.hops = [(k, k - 1) for k in range(shards - 1, 0, -1)]
            else:
                self.hops = [(k, k + 1) for k in range(shards - 1)]
            self.landed = []

        def start(self, token=None):
            got = after(self.got, token)
            self.zero = jnp.where(first, self.mine, got)
            self.one = jnp.where(first, got, self.mine)
            if self.backward:
                self.total = self.g0 * self.one + self.zero
            else:
                self.total = self.g1 * self.zero + self.one

        def hop(self, index, token=None):
            if index == 0:
                self.start(token)
                self.sent = self.total
            else:
                self.settle(token)
                self.sent = self.both * self.state + self.total
            self.landed.append(lax.ppermute(self.sent, "seq", [self.hops[index]]))

        def settle(self, token=None):
            self.landed[-1] = after(self.landed[-1], token)
            self.state = sum(self.landed[1:], self.landed[0])

        def finish(self, token=None):
            self.settle(token)
            state = self.state
            if self.backward:
                inner = self.g1 * state + self.one
                keep, send = jnp.where(first, inner, state), jnp.where(first, state, inner)
            else:
                inner = self.g0 * state + self.zero
                keep, send = jnp.where(first, state, inner), jnp.where(first, inner, state)
            return keep, lax.ppermute(send, "ctx", swap)

    def inside_of(group, token):
        return call(
            inside_kernel, group,
            ["rows"] * 3 + ["run", "table", "bias", "bias", "bias"],
            ["states"] + ["headed"] * 5,
            (states_shape, headed(F32), headed(BF16), headed(BF16), headed(BF16), headed(BF16)),
            (query_in, key_in, value_in, run, table, weight_bias, enter_bias, leave_bias),
            "inside", 4, 10,
            stay=("rows",),
            tokens=[token],
        )

    hops = range(shards - 1)
    carries = [Carry(group, updates[2 * group], updates[2 * group + 1], False) for group in range(groups)]
    insides = []
    token = None
    for index in hops:
        for carry in carries:
            carry.hop(index, token)
            token = carry.sent
        while index == min(1, shards - 2) and len(insides) < groups:
            insides.append(inside_of(len(insides), token))
            token = insides[-1][0]

    normed = None
    incoming, middles, backs = [], [], []
    query_gradient = None
    dattends = []

    def query_of(group, token):
        return call(
            query_kernel, group,
            ["rows", "rows", "headed", "run", "table", "bias", "bias", "states", "mine", "other"],
            ["rows", "headed"],
            (rows_shape, headed(BF16)),
            (
                key_in, value_in, middles[group][0], run, table, weight_bias, enter_bias, insides[group][0],
                *incoming[group],
            ),
            "query", 3, 8,
            aliases=(query_gradient,),
            tokens=[token],
        )

    for group in range(groups):
        incoming.append(carries[group].finish(token))
        prefix, inside, qd = insides[group][:3]
        normed, grad, suffix, mine, other = call(
            forward_kernel, group,
            ["headed", "headed", "rows", "table", "states", "mine", "other"],
            ["rows", "headed", "states", "mine", "other"],
            (rows_shape, headed(BF16), states_shape, part_shape, part_shape),
            (inside, qd, out_grad, table, prefix, *incoming[group]),
            "forward", 2, 8,
            aliases=(normed,),
            tokens=[backs[-1].sent] if backs else [],
        )
        token = mine
        middles.append((grad, suffix))
        backs.append(Carry(group, mine, other, True))
        if group < groups - 1:
            query_gradient, dattend = query_of(group, token)
            dattends.append(dattend)
            token = dattend
        if group == 0:
            backs[0].hop(0)

    for index in hops:
        for place, back in enumerate(backs):
            ahead = index + 1 if place == 0 else index
            if ahead in hops:
                back.hop(ahead, token)
                token = back.sent
        while index == min(1, shards - 2) and len(dattends) < groups:
            query_gradient, dattend = query_of(len(dattends), token)
            dattends.append(dattend)
            token = dattend
    grads = (None, None)
    for group in range(groups):
        grad, suffix = middles[group]
        kd, vd, attend = insides[group][3:]
        grads = call(
            backward_kernel, group,
            ["rows"] + ["headed"] * 5 + ["table", "states", "mine", "other"],
            ["rows", "rows"],
            (rows_shape, rows_shape),
            (query_in, grad, attend, dattends[group], kd, vd, table, suffix, *backs[group].finish(token)),
            "backward", 4, 10,
            aliases=grads,
        )
        token = grads[0]
    return (normed, query_gradient, *grads)


def solution(mesh):
    rows = P(("groups", "seq", "ctx"), "tensor")
    return jax.shard_map(
        local,
        mesh=mesh,
        in_specs=(rows, rows, rows, P("tensor", ("groups", "seq", "ctx")), P(("groups", "seq", "ctx")), rows),
        out_specs=(rows, rows, rows, rows),
        check_vma=False,
    )
```
